512 devices in a mesh: wide: 64 (over z, y_lo, core), narrow: 8 (over y_hi, x).
Axes of the slice: x: 4, y: 8 (y_hi: 2, y_lo: 4; y = y_hi * 4 + y_lo), z: 8, core: 2. Of those that a mesh axis runs over, the one named last changes fastest.
Arguments:
- volume: float32 [256, 128, 1024], P('wide', 'narrow'), may hold values from -12 to 12
Outputs:
- smoothed: float32 [256, 128, 1024], P('wide', 'narrow')
The draws below stay inside these ranges and needn't reach their ends.
All inputs are finite; a program needn't handle non-finite values.
Results may differ from the reference program's by a relative error of at most 0.00019.
Values sent between devices are 32-bit elements; how exact they have to be, the bound alone decides.
No kernel may reach another device: no remote copies, remote signals or barrier semaphores. Data moves between devices by JAX's collectives and lax.ppermute only.
A program may use at most 64 MiB of HBM per device.

```python
import jax
import jax.numpy as jnp
from jax import lax

NT = 1024
NI = 256
NC = 128


def draw_volume(key, part):
    key = jax.random.fold_in(key, 11)
    return 3.0 * jax.random.truncated_normal(key, -4.0, 4.0, (NI, NC, NT), jnp.float32)


def setup_inputs(seed: int = 0) -> dict:
    key_list = jax.random.split(jax.random.key(seed), 2)
    return {
        "volume": draw_volume(jax.random.fold_in(key_list[1], 71), 0),
    }


step_weight = 300.0
contrast_sq = 9.0

def solve_last(values, cond):
    between = 0.5 * (cond[..., :-1] + cond[..., 1:])
    edge = jnp.zeros_like(cond[..., :1])
    lower = jnp.concatenate([edge, -step_weight * between], -1)
    upper = jnp.concatenate([-step_weight * between, edge], -1)
    diag = 1.0 - lower - upper
    return lax.linalg.tridiagonal_solve(lower, diag, upper, values[..., None])[..., 0]

def solve_rows(values, cond):
    return lax.map(lambda pair: solve_last(pair[0], pair[1]), (values, cond))

def reference(volume):
    padded = jnp.pad(volume, 1, mode='edge')
    power = (0.5 * (padded[2:, 1:-1, 1:-1] - padded[:-2, 1:-1, 1:-1])) ** 2
    power = power + (0.5 * (padded[1:-1, 2:, 1:-1] - padded[1:-1, :-2, 1:-1])) ** 2
    power = power + (0.5 * (padded[1:-1, 1:-1, 2:] - padded[1:-1, 1:-1, :-2])) ** 2
    cond = 1.0 / (1.0 + power / contrast_sq)
    along_time = solve_rows(volume, cond)
    moved = solve_rows(jnp.transpose(volume, (1, 2, 0)), jnp.transpose(cond, (1, 2, 0)))
    along_inline = jnp.transpose(moved, (2, 0, 1))
    moved = solve_rows(jnp.transpose(volume, (0, 2, 1)), jnp.transpose(cond, (0, 2, 1)))
    along_cross = jnp.transpose(moved, (0, 2, 1))
    return (along_inline + along_cross + along_time) / 3.0
```

```python
import jax
import jax.numpy as jnp
from jax import lax
from jax.experimental import pallas as pl
from jax.experimental.pallas import tpu as pltpu
from jax.sharding import PartitionSpec as P

half_weight = 150.0
contrast_sq = 9.0

WIDE = 64
NARROW = 8
INL = 4
CRS = 16
NT = 1024
LANES = 128
TILES = NT // LANES
ROWS = INL * TILES
GROUP = 8
PORTS = 7


def condense(mass, rhs, link):
    mass, rhs, right = list(mass), list(rhs), list(link)
    alive, steps = list(range(len(mass))), []
    while len(alive) > 2:
        gone = set()
        for at in range(1, len(alive) - 1, 2):
            l, k, r = alive[at - 1 : at + 2]
            inverse = 1.0 / (right[l] + right[k] + mass[k])
            to_left, to_right = right[l] * inverse, right[k] * inverse
            mass[l] = mass[l] + to_left * mass[k]
            rhs[l] = rhs[l] + to_left * rhs[k]
            mass[r] = mass[r] + to_right * mass[k]
            rhs[r] = rhs[r] + to_right * rhs[k]
            right[l] = to_left * right[k]
            steps.append((l, k, r, to_left, to_right, rhs[k] * inverse))
            gone.add(k)
        alive = [k for k in alive if k not in gone]
    return mass[0], rhs[0], mass[-1], rhs[-1], right[0], steps


def expand(first, last, steps, count):
    x = [None] * count
    x[0], x[-1] = first, last
    for l, k, r, to_left, to_right, base in reversed(steps):
        x[k] = base + to_left * x[l] + to_right * x[r]
    return x


def links(cond):
    return [half_weight * (a + b) for a, b in zip(cond[:-1], cond[1:])]


def halving(mass, rhs, before, after, shift, count):
    step = 1
    while step < count:
        inverse = 1.0 / (before + after + mass)
        to_left, to_right = before * inverse, after * inverse
        across = to_left * after
        mass, rhs = (
            mass + shift(to_right * mass, step) + shift(to_left * mass, -step),
            rhs + shift(to_right * rhs, step) + shift(to_left * rhs, -step),
        )
        before, after = shift(across, step), shift(across, -step)
        step *= 2
    return rhs / mass


def iota(shape, dim):
    return lax.broadcasted_iota(jnp.int32, shape, dim)


def lane_tile(t):
    return slice(t * LANES, (t + 1) * LANES)


def prepare_kernel(
    axes, vol, before, after, left, right, cond, wide_out, narrow_out, cells_v, cells_c
):
    wide_axes, narrow_axes = axes
    wide_rank, narrow_rank = lax.axis_index(wide_axes), lax.axis_index(narrow_axes)
    col = iota((CRS, NT), 1)
    row = iota((CRS, NT), 0)
    for i in range(INL):
        here = vol[i]
        if i == 0:
            up = jnp.where(wide_rank == 0, here, before[0])
        else:
            up = vol[i - 1]
        if i == INL - 1:
            down = jnp.where(wide_rank == WIDE - 1, here, after[0])
        else:
            down = vol[i + 1]
        power = (0.5 * (down - up)) ** 2
        edge = jnp.where(narrow_rank == 0, here[:1], left[i])
        lower = jnp.where(row == 0, edge, pltpu.roll(here, 1, 0))
        edge = jnp.where(narrow_rank == NARROW - 1, here[CRS - 1 :], right[i])
        upper = jnp.where(row == CRS - 1, edge, pltpu.roll(here, CRS - 1, 0))
        power = power + (0.5 * (upper - lower)) ** 2
        earlier = jnp.where(col == 0, here, pltpu.roll(here, 1, 1))
        later = jnp.where(col == NT - 1, here, pltpu.roll(here, NT - 1, 1))
        power = power + (0.5 * (later - earlier)) ** 2
        value = contrast_sq / (contrast_sq + power)
        cond[i] = value
        for t in range(TILES):
            where = pl.ds(i * TILES + t, CRS, stride=ROWS)
            cells_v[where, :] = here[:, lane_tile(t)]
            cells_c[where, :] = value[:, lane_tile(t)]
    ones = jnp.ones((ROWS, LANES), jnp.float32)
    v = [cells_v[pl.ds(c * ROWS, ROWS), :] for c in range(CRS)]
    k = [cells_c[pl.ds(c * ROWS, ROWS), :] for c in range(CRS)]
    m0, d0, m1, d1, g, _ = condense([ones] * CRS, v, links(k))
    for p, value in enumerate((g, m0, m1, d0, d1, k[0], k[-1])):
        narrow_out[p * ROWS : (p + 1) * ROWS, :] = value
    ones = jnp.ones((GROUP, LANES), jnp.float32)
    for t in range(TILES):
        for u in range(CRS // GROUP):
            at = (slice(u * GROUP, (u + 1) * GROUP), lane_tile(t))
            v = [vol[(i, *at)] for i in range(INL)]
            k = [cond[(i, *at)] for i in range(INL)]
            m0, d0, m1, d1, g, _ = condense([ones] * INL, v, links(k))
            for p, value in enumerate((g, m0, m1, d0, d1, k[0], k[-1])):
                start = t * GROUP * 2 * PORTS + p * 2 + u
                wide_out[pl.ds(start, GROUP, stride=2 * PORTS), :] = value


def sublane_shift(x, s):
    return pltpu.roll(x, s % GROUP, 0)


def wide_kernel(ports, out):
    part = WIDE // GROUP
    sub = iota((GROUP, LANES), 0)
    zero = jnp.zeros((GROUP, LANES), jnp.float32)
    for u in range(2):

        def port(p, j):
            return ports[pl.ds(j * 2 * PORTS + p * 2 + u, GROUP, stride=part * 2 * PORTS), :]

        last_cond = sublane_shift(port(6, part - 1), 1)
        mass, rhs, link = [zero], [zero], []
        for j in range(part):
            joined = half_weight * (last_cond + port(5, j))
            if j == 0:
                joined = jnp.where(sub == 0, 0.0, joined)
            link += [joined, port(0, j)]
            mass += [port(1, j), port(2, j)]
            rhs += [port(3, j), port(4, j)]
            last_cond = port(6, j)
        count = len(mass)
        m0, d0, m1, d1, g, steps = condense(mass, rhs, link)
        last = halving(
            m1 + sublane_shift(m0, -1),
            d1 + sublane_shift(d0, -1),
            g,
            sublane_shift(g, -1),
            sublane_shift,
            GROUP,
        )
        x = expand(sublane_shift(last, 1), last, steps, count)
        for j in range(part):
            for e in range(2):
                out[pl.ds(j * 4 + e * 2 + u, GROUP, stride=part * 4), :] = x[1 + 2 * j + e]


def time_kernel(vol, cond, out, cells_v, cells_c, link_s, tmp):
    lines = INL * CRS
    half = NT // 2
    blocks = half // LANES
    for b in range(blocks):
        for source, cells in ((vol, cells_v), (cond, cells_c)):
            stacked = jnp.concatenate(
                [
                    source[:, :, b * LANES : (b + 1) * LANES].reshape(lines, LANES),
                    source[:, :, half + b * LANES : half + (b + 1) * LANES].reshape(lines, LANES),
                ],
                0,
            )
            cells[b * LANES : (b + 1) * LANES, :] = stacked.T
    lane = iota((GROUP, LANES), 1)
    sub = iota((GROUP, LANES), 0)
    low = lane < lines

    def swap(x):
        return pltpu.roll(x, lines, 1)

    for s in range(half // GROUP):
        here = cells_c[s * GROUP : (s + 1) * GROUP, :]
        if s:
            edge = cells_c[s * GROUP - 1 : s * GROUP, :]
        else:
            edge = swap(cells_c[half - GROUP : half, :])[GROUP - 1 :]
        value = half_weight * (here + jnp.where(sub == 0, edge, pltpu.roll(here, 1, 0)))
        if s == 0:
            value = jnp.where((sub == 0) & low, 0.0, value)
        link_s[s * GROUP : (s + 1) * GROUP, :] = value

    def chain_shift(x, s):
        n = x.shape[0]
        if abs(s) == n:
            return swap(x)
        rolled = pltpu.roll(x, s % n, 0)
        place = iota(x.shape, 0)
        wrapped = place < s if s > 0 else place >= n + s
        return jnp.where(wrapped, swap(rolled), rolled)

    runs = half // GROUP
    zero = jnp.zeros((runs, LANES), jnp.float32)
    ones = jnp.ones((runs, LANES), jnp.float32)
    v = [cells_v[pl.ds(k, runs, stride=GROUP), :] for k in range(GROUP)]
    link = [link_s[pl.ds(k, runs, stride=GROUP), :] for k in range(GROUP)]
    m0, d0, m1, d1, g, steps = condense([zero] + [ones] * GROUP, [zero] + v, link)
    tmp[0] = m1 + chain_shift(m0, -1)
    tmp[1] = d1 + chain_shift(d0, -1)
    tmp[2] = g
    zero = jnp.zeros((GROUP, LANES), jnp.float32)

    def take(p):
        return [tmp[p, pl.ds(k, GROUP, stride=GROUP), :] for k in range(GROUP)]

    m0, d0, m1, d1, g, inner = condense([zero] + take(0), [zero] + take(1), take(2))
    last = halving(
        m1 + chain_shift(m0, -1),
        d1 + chain_shift(d0, -1),
        g,
        chain_shift(g, -1),
        chain_shift,
        2 * GROUP,
    )
    x = expand(chain_shift(last, 1), last, inner, GROUP + 1)
    for k in range(GROUP):
        tmp[0, pl.ds(k, GROUP, stride=GROUP), :] = x[k + 1]
    last = tmp[0]
    x = expand(chain_shift(last, 1), last, steps, GROUP + 1)
    for k in range(GROUP):
        cells_v[pl.ds(k, runs, stride=GROUP), :] = x[k + 1]
    for b in range(blocks):
        turned = cells_v[b * LANES : (b + 1) * LANES, :].T
        for h in range(2):
            out[:, :, h * half + b * LANES : h * half + (b + 1) * LANES] = turned[
                h * lines : (h + 1) * lines
            ].reshape(INL, CRS, LANES)


def cross_kernel(axes, gathered, cells_v, cells_c, timed, out, ends, cells_x):
    rank = lax.axis_index(axes[1])
    ports = [
        [gathered[n, p * ROWS : (p + 1) * ROWS, :] for p in range(PORTS)] for n in range(NARROW)
    ]
    mass, rhs, link = [], [], []
    for n, (g, m0, m1, d0, d1, _, _) in enumerate(ports):
        mass += [m0, m1]
        rhs += [d0, d1]
        link.append(g)
        if n < NARROW - 1:
            link.append(half_weight * (ports[n][6] + ports[n + 1][5]))
    m0, d0, m1, d1, g, steps = condense(mass, rhs, link)
    inverse = 1.0 / (m0 * m1 + g * (m0 + m1))
    first = (d0 * (m1 + g) + g * d1) * inverse
    last = (d1 * (m0 + g) + g * d0) * inverse
    for n, value in enumerate(expand(first, last, steps, 2 * NARROW)):
        ends[n] = value
    v = [cells_v[pl.ds(c * ROWS, ROWS), :] for c in range(CRS)]
    k = [cells_c[pl.ds(c * ROWS, ROWS), :] for c in range(CRS)]
    ones = jnp.ones((ROWS, LANES), jnp.float32)
    _, _, _, _, _, steps = condense([ones] * CRS, v, links(k))
    x = expand(ends[2 * rank], ends[2 * rank + 1], steps, CRS)
    for c in range(CRS):
        cells_x[c * ROWS : (c + 1) * ROWS, :] = x[c]
    for i in range(INL):
        for t in range(TILES):
            out[i, :, lane_tile(t)] = (
                timed[i, :, lane_tile(t)] + cells_x[pl.ds(i * TILES + t, CRS, stride=ROWS), :]
            )


def finish_kernel(vol, cond, ends, others, out):
    ones = jnp.ones((GROUP, LANES), jnp.float32)
    for t in range(TILES):
        for u in range(CRS // GROUP):
            at = (slice(u * GROUP, (u + 1) * GROUP), lane_tile(t))
            v = [vol[(i, *at)] for i in range(INL)]
            k = [cond[(i, *at)] for i in range(INL)]
            steps = condense([ones] * INL, v, links(k))[-1]
            first = ends[pl.ds(t * GROUP * 4 + u, GROUP, stride=4), :]
            last = ends[pl.ds(t * GROUP * 4 + 2 + u, GROUP, stride=4), :]
            for i, x in enumerate(expand(first, last, steps, INL)):
                out[(i, *at)] = (x + others[(i, *at)]) * (1.0 / 3.0)


def f32(*shape):
    return jax.ShapeDtypeStruct(shape, jnp.float32)


def call(kernel, out, *args, scratch=()):
    return pl.pallas_call(
        kernel,
        out_shape=out,
        scratch_shapes=[pltpu.VMEM(s, jnp.float32) for s in scratch],
        compiler_params=pltpu.CompilerParams(vmem_limit_bytes=16 * 2**20),
    )(*args)


def per_device(axes, volume):
    wide_axes, narrow_axes = axes

    def neighbour(x, axis, count, step):
        pairs = [(i, i + step) for i in range(count) if 0 <= i + step < count]
        return lax.ppermute(x, axis, pairs)

    before = neighbour(volume[-1:], wide_axes, WIDE, 1)
    after = neighbour(volume[:1], wide_axes, WIDE, -1)
    left = neighbour(volume[:, -1:], narrow_axes, NARROW, 1)
    right = neighbour(volume[:, :1], narrow_axes, NARROW, -1)
    cells = CRS * ROWS
    cond, wide_ports, narrow_ports, cells_v, cells_c = call(
        lambda *refs: prepare_kernel(axes, *refs),
        (
            f32(INL, CRS, NT),
            f32(WIDE * PORTS * 2, LANES),
            f32(PORTS * ROWS, LANES),
            f32(cells, LANES),
            f32(cells, LANES),
        ),
        volume,
        before,
        after,
        left,
        right,
    )
    lines = lax.all_to_all(
        wide_ports.reshape(WIDE, PORTS, 2, LANES), wide_axes, split_axis=0, concat_axis=0, tiled=True
    )
    spread = jnp.broadcast_to(narrow_ports[None], (NARROW, PORTS * ROWS, LANES))
    gathered = lax.all_to_all(spread, narrow_axes, split_axis=0, concat_axis=0, tiled=True)
    timed = call(
        time_kernel,
        f32(INL, CRS, NT),
        volume,
        cond,
        scratch=(
            (NT // 2, LANES),
            (NT // 2, LANES),
            (NT // 2, LANES),
            (3, NT // 2 // GROUP, LANES),
        ),
    )
    solved = call(
        wide_kernel, f32(WIDE * 4, LANES), lines.reshape(WIDE * PORTS * 2, LANES)
    )
    ends = lax.all_to_all(
        solved.reshape(WIDE, 2, 2, LANES), wide_axes, split_axis=0, concat_axis=0, tiled=True
    )
    others = call(
        lambda *refs: cross_kernel(axes, *refs),
        f32(INL, CRS, NT),
        gathered,
        cells_v,
        cells_c,
        timed,
        scratch=((2 * NARROW, ROWS, LANES), (cells, LANES)),
    )
    return call(
        finish_kernel, f32(INL, CRS, NT), volume, cond, ends.reshape(WIDE * 4, LANES), others
    )


def solution(mesh):
    axes = ("wide", "narrow")
    return jax.shard_map(
        lambda volume: per_device(axes, volume),
        mesh=mesh,
        in_specs=(P("wide", "narrow", None),),
        out_specs=P("wide", "narrow", None),
        check_vma=False,
    )
```

```python
import jax
import jax.numpy as jnp
from jax import lax
from jax.experimental import pallas as pl
from jax.experimental.pallas import tpu as pltpu
from jax.sharding import PartitionSpec as P

half_weight = 150.0
contrast_sq = 9.0

WIDE = 64
NARROW = 8
INL = 4
CRS = 16
NT = 1024
LANES = 128
TILES = NT // LANES
ROWS = INL * TILES
GROUP = 8
PORTS = 7
RUN = 4


def condense(mass, rhs, link):
    mass, rhs, right = list(mass), list(rhs), list(link)
    alive, steps = list(range(len(mass))), []
    while len(alive) > 2:
        gone = set()
        for at in range(1, len(alive) - 1, 2):
            l, k, r = alive[at - 1 : at + 2]
            inverse = 1.0 / (right[l] + right[k] + mass[k])
            to_left, to_right = right[l] * inverse, right[k] * inverse
            mass[l] = mass[l] + to_left * mass[k]
            rhs[l] = rhs[l] + to_left * rhs[k]
            mass[r] = mass[r] + to_right * mass[k]
            rhs[r] = rhs[r] + to_right * rhs[k]
            right[l] = to_left * right[k]
            steps.append((l, k, r, to_left, to_right, rhs[k] * inverse))
            gone.add(k)
        alive = [k for k in alive if k not in gone]
    return mass[0], rhs[0], mass[-1], rhs[-1], right[0], steps


def expand(first, last, steps, count):
    x = [None] * count
    x[0], x[-1] = first, last
    for l, k, r, to_left, to_right, base in reversed(steps):
        x[k] = base + to_left * x[l] + to_right * x[r]
    return x


def links(cond):
    return [half_weight * (a + b) for a, b in zip(cond[:-1], cond[1:])]


def halving(mass, rhs, before, after, shift, count):
    step = 1
    while step < count:
        inverse = 1.0 / (before + after + mass)
        to_left, to_right = before * inverse, after * inverse
        across = to_left * after
        mass, rhs = (
            mass + shift(to_right * mass, step) + shift(to_left * mass, -step),
            rhs + shift(to_right * rhs, step) + shift(to_left * rhs, -step),
        )
        before, after = shift(across, step), shift(across, -step)
        step *= 2
    return rhs / mass


def iota(shape, dim):
    return lax.broadcasted_iota(jnp.int32, shape, dim)


def lane_tile(t):
    return slice(t * LANES, (t + 1) * LANES)


def prepare_kernel(
    axes, vol, before, after, left, right, cond, wide_out, narrow_out, cells_v, cells_c
):
    wide_axes, narrow_axes = axes
    wide_rank, narrow_rank = lax.axis_index(wide_axes), lax.axis_index(narrow_axes)
    col = iota((CRS, NT), 1)
    row = iota((CRS, NT), 0)
    for i in range(INL):
        here = vol[i]
        if i == 0:
            up = jnp.where(wide_rank == 0, here, before[0])
        else:
            up = vol[i - 1]
        if i == INL - 1:
            down = jnp.where(wide_rank == WIDE - 1, here, after[0])
        else:
            down = vol[i + 1]
        power = (0.5 * (down - up)) ** 2
        edge = jnp.where(narrow_rank == 0, here[:1], left[i])
        lower = jnp.where(row == 0, edge, pltpu.roll(here, 1, 0))
        edge = jnp.where(narrow_rank == NARROW - 1, here[CRS - 1 :], right[i])
        upper = jnp.where(row == CRS - 1, edge, pltpu.roll(here, CRS - 1, 0))
        power = power + (0.5 * (upper - lower)) ** 2
        earlier = jnp.where(col == 0, here, pltpu.roll(here, 1, 1))
        later = jnp.where(col == NT - 1, here, pltpu.roll(here, NT - 1, 1))
        power = power + (0.5 * (later - earlier)) ** 2
        value = contrast_sq / (contrast_sq + power)
        cond[i] = value
        for t in range(TILES):
            where = pl.ds(i * TILES + t, CRS, stride=ROWS)
            cells_v[where, :] = here[:, lane_tile(t)]
            cells_c[where, :] = value[:, lane_tile(t)]
    ones = jnp.ones((ROWS, LANES), jnp.float32)
    v = [cells_v[pl.ds(c * ROWS, ROWS), :] for c in range(CRS)]
    k = [cells_c[pl.ds(c * ROWS, ROWS), :] for c in range(CRS)]
    m0, d0, m1, d1, g, _ = condense([ones] * CRS, v, links(k))
    for p, value in enumerate((g, m0, m1, d0, d1, k[0], k[-1])):
        narrow_out[p * ROWS : (p + 1) * ROWS, :] = value
    ones = jnp.ones((GROUP, LANES), jnp.float32)
    for t in range(TILES):
        for u in range(CRS // GROUP):
            at = (slice(u * GROUP, (u + 1) * GROUP), lane_tile(t))
            v = [vol[(i, *at)] for i in range(INL)]
            k = [cond[(i, *at)] for i in range(INL)]
            m0, d0, m1, d1, g, _ = condense([ones] * INL, v, links(k))
            for p, value in enumerate((g, m0, m1, d0, d1, k[0], k[-1])):
                start = t * GROUP * 2 * PORTS + p * 2 + u
                wide_out[pl.ds(start, GROUP, stride=2 * PORTS), :] = value


def sublane_shift(x, s):
    return pltpu.roll(x, s % GROUP, 0)


def wide_kernel(ports, out):
    part = WIDE // GROUP
    sub = iota((GROUP, LANES), 0)
    zero = jnp.zeros((GROUP, LANES), jnp.float32)
    for u in range(2):

        def port(p, j):
            return ports[pl.ds(j * 2 * PORTS + p * 2 + u, GROUP, stride=part * 2 * PORTS), :]

        last_cond = sublane_shift(port(6, part - 1), 1)
        mass, rhs, link = [zero], [zero], []
        for j in range(part):
            joined = half_weight * (last_cond + port(5, j))
            if j == 0:
                joined = jnp.where(sub == 0, 0.0, joined)
            link += [joined, port(0, j)]
            mass += [port(1, j), port(2, j)]
            rhs += [port(3, j), port(4, j)]
            last_cond = port(6, j)
        count = len(mass)
        m0, d0, m1, d1, g, steps = condense(mass, rhs, link)
        last = halving(
            m1 + sublane_shift(m0, -1),
            d1 + sublane_shift(d0, -1),
            g,
            sublane_shift(g, -1),
            sublane_shift,
            GROUP,
        )
        x = expand(sublane_shift(last, 1), last, steps, count)
        for j in range(part):
            for e in range(2):
                out[pl.ds(j * 4 + e * 2 + u, GROUP, stride=part * 4), :] = x[1 + 2 * j + e]


def time_kernel(vol, cond, out, cells_v, cells_c, link_s, tmp):
    lines = INL * CRS
    half = NT // 2
    blocks = half // LANES
    for b in range(blocks):
        for source, cells in ((vol, cells_v), (cond, cells_c)):
            stacked = jnp.concatenate(
                [
                    source[:, :, b * LANES : (b + 1) * LANES].reshape(lines, LANES),
                    source[:, :, half + b * LANES : half + (b + 1) * LANES].reshape(lines, LANES),
                ],
                0,
            )
            cells[b * LANES : (b + 1) * LANES, :] = stacked.T
    lane = iota((GROUP, LANES), 1)
    sub = iota((GROUP, LANES), 0)
    low = lane < lines

    def swap(x):
        return pltpu.roll(x, lines, 1)

    for s in range(half // GROUP):
        here = cells_c[s * GROUP : (s + 1) * GROUP, :]
        if s:
            edge = cells_c[s * GROUP - 1 : s * GROUP, :]
        else:
            edge = swap(cells_c[half - GROUP : half, :])[GROUP - 1 :]
        value = half_weight * (here + jnp.where(sub == 0, edge, pltpu.roll(here, 1, 0)))
        if s == 0:
            value = jnp.where((sub == 0) & low, 0.0, value)
        link_s[s * GROUP : (s + 1) * GROUP, :] = value

    def chain_shift(x, s):
        n = x.shape[0]
        if abs(s) == n:
            return swap(x)
        rolled = pltpu.roll(x, s % n, 0)
        place = iota(x.shape, 0)
        wrapped = place < s if s > 0 else place >= n + s
        return jnp.where(wrapped, swap(rolled), rolled)

    runs = half // GROUP
    zero = jnp.zeros((runs, LANES), jnp.float32)
    ones = jnp.ones((runs, LANES), jnp.float32)
    v = [cells_v[pl.ds(k, runs, stride=GROUP), :] for k in range(GROUP)]
    link = [link_s[pl.ds(k, runs, stride=GROUP), :] for k in range(GROUP)]
    m0, d0, m1, d1, g, steps = condense([zero] + [ones] * GROUP, [zero] + v, link)
    tmp[0] = m1 + chain_shift(m0, -1)
    tmp[1] = d1 + chain_shift(d0, -1)
    tmp[2] = g
    zero = jnp.zeros((GROUP, LANES), jnp.float32)

    def take(p):
        return [tmp[p, pl.ds(k, GROUP, stride=GROUP), :] for k in range(GROUP)]

    m0, d0, m1, d1, g, inner = condense([zero] + take(0), [zero] + take(1), take(2))
    last = halving(
        m1 + chain_shift(m0, -1),
        d1 + chain_shift(d0, -1),
        g,
        chain_shift(g, -1),
        chain_shift,
        2 * GROUP,
    )
    x = expand(chain_shift(last, 1), last, inner, GROUP + 1)
    for k in range(GROUP):
        tmp[0, pl.ds(k, GROUP, stride=GROUP), :] = x[k + 1]
    last = tmp[0]
    x = expand(chain_shift(last, 1), last, steps, GROUP + 1)
    for k in range(GROUP):
        cells_v[pl.ds(k, runs, stride=GROUP), :] = x[k + 1]
    for b in range(blocks):
        turned = cells_v[b * LANES : (b + 1) * LANES, :].T
        for h in range(2):
            out[:, :, h * half + b * LANES : h * half + (b + 1) * LANES] = turned[
                h * lines : (h + 1) * lines
            ].reshape(INL, CRS, LANES)


def ports_of(ref):
    return [ref[p * ROWS : (p + 1) * ROWS, :] for p in range(PORTS)]


def chain_of(ports):
    mass, rhs, link = [], [], []
    for n, (g, m0, m1, d0, d1, _, _) in enumerate(ports):
        mass += [m0, m1]
        rhs += [d0, d1]
        link.append(g)
        if n < len(ports) - 1:
            link.append(half_weight * (ports[n][6] + ports[n + 1][5]))
    return mass, rhs, link


def merge_kernel(axes, own, by1, by2, by3, held, merged):
    place = lax.rem(lax.axis_index(axes[1]), RUN)
    for step, ref in enumerate((own, by1, by2, by3)):
        held[place ^ step] = ref[...]
    ports = [ports_of(held.at[n]) for n in range(RUN)]
    m0, d0, m1, d1, g, _ = condense(*chain_of(ports))
    for p, value in enumerate((g, m0, m1, d0, d1, ports[0][5], ports[-1][6])):
        merged[p * ROWS : (p + 1) * ROWS, :] = value


def cross_kernel(axes, held, merged, other, cells_v, cells_c, timed, out, ends, cells_x):
    rank = lax.axis_index(axes[1])
    place, high = lax.rem(rank, RUN), rank >= RUN
    own, far = ports_of(merged), ports_of(other)
    pair = [
        [jnp.where(high, b, a) for a, b in zip(own, far)],
        [jnp.where(high, a, b) for a, b in zip(own, far)],
    ]
    m0, d0, m1, d1, g, steps = condense(*chain_of(pair))
    inverse = 1.0 / (m0 * m1 + g * (m0 + m1))
    first = (d0 * (m1 + g) + g * d1) * inverse
    last = (d1 * (m0 + g) + g * d0) * inverse
    x = expand(first, last, steps, 4)
    first, last = jnp.where(high, x[2], x[0]), jnp.where(high, x[3], x[1])
    steps = condense(*chain_of([ports_of(held.at[n]) for n in range(RUN)]))[-1]
    for n, value in enumerate(expand(first, last, steps, 2 * RUN)):
        ends[n] = value
    v = [cells_v[pl.ds(c * ROWS, ROWS), :] for c in range(CRS)]
    k = [cells_c[pl.ds(c * ROWS, ROWS), :] for c in range(CRS)]
    ones = jnp.ones((ROWS, LANES), jnp.float32)
    steps = condense([ones] * CRS, v, links(k))[-1]
    x = expand(ends[2 * place], ends[2 * place + 1], steps, CRS)
    for c in range(CRS):
        cells_x[c * ROWS : (c + 1) * ROWS, :] = x[c]
    for i in range(INL):
        for t in range(TILES):
            out[i, :, lane_tile(t)] = (
                timed[i, :, lane_tile(t)] + cells_x[pl.ds(i * TILES + t, CRS, stride=ROWS), :]
            )


def finish_kernel(vol, cond, ends, others, out):
    ones = jnp.ones((GROUP, LANES), jnp.float32)
    for t in range(TILES):
        for u in range(CRS // GROUP):
            at = (slice(u * GROUP, (u + 1) * GROUP), lane_tile(t))
            v = [vol[(i, *at)] for i in range(INL)]
            k = [cond[(i, *at)] for i in range(INL)]
            steps = condense([ones] * INL, v, links(k))[-1]
            first = ends[pl.ds(t * GROUP * 4 + u, GROUP, stride=4), :]
            last = ends[pl.ds(t * GROUP * 4 + 2 + u, GROUP, stride=4), :]
            for i, x in enumerate(expand(first, last, steps, INL)):
                out[(i, *at)] = (x + others[(i, *at)]) * (1.0 / 3.0)


def f32(*shape):
    return jax.ShapeDtypeStruct(shape, jnp.float32)


def call(kernel, out, *args, scratch=()):
    return pl.pallas_call(
        kernel,
        out_shape=out,
        scratch_shapes=[pltpu.VMEM(s, jnp.float32) for s in scratch],
        compiler_params=pltpu.CompilerParams(vmem_limit_bytes=16 * 2**20),
    )(*args)


def per_device(axes, volume):
    wide_axes, narrow_axes = axes

    def neighbour(x, axis, count, step):
        pairs = [(i, i + step) for i in range(count) if 0 <= i + step < count]
        return lax.ppermute(x, axis, pairs)

    before = neighbour(volume[-1:], wide_axes, WIDE, 1)
    after = neighbour(volume[:1], wide_axes, WIDE, -1)
    left = neighbour(volume[:, -1:], narrow_axes, NARROW, 1)
    right = neighbour(volume[:, :1], narrow_axes, NARROW, -1)
    cells = CRS * ROWS
    cond, wide_ports, narrow_ports, cells_v, cells_c = call(
        lambda *refs: prepare_kernel(axes, *refs),
        (
            f32(INL, CRS, NT),
            f32(WIDE * PORTS * 2, LANES),
            f32(PORTS * ROWS, LANES),
            f32(cells, LANES),
            f32(cells, LANES),
        ),
        volume,
        before,
        after,
        left,
        right,
    )
    lines = lax.all_to_all(
        wide_ports.reshape(WIDE, PORTS, 2, LANES), wide_axes, split_axis=0, concat_axis=0, tiled=True
    )

    def swapped(x, step):
        return lax.ppermute(x, narrow_axes, [(n, n ^ step) for n in range(NARROW)])

    held, merged = call(
        lambda *refs: merge_kernel(axes, *refs),
        (f32(RUN, PORTS * ROWS, LANES), f32(PORTS * ROWS, LANES)),
        narrow_ports,
        *[swapped(narrow_ports, step) for step in range(1, RUN)],
    )
    other = swapped(merged, RUN)
    timed = call(
        time_kernel,
        f32(INL, CRS, NT),
        volume,
        cond,
        scratch=(
            (NT // 2, LANES),
            (NT // 2, LANES),
            (NT // 2, LANES),
            (3, NT // 2 // GROUP, LANES),
        ),
    )
    lines, held, timed = lax.optimization_barrier((lines, held, timed))
    solved = call(
        wide_kernel, f32(WIDE * 4, LANES), lines.reshape(WIDE * PORTS * 2, LANES)
    )
    ends = lax.all_to_all(
        solved.reshape(WIDE, 2, 2, LANES), wide_axes, split_axis=0, concat_axis=0, tiled=True
    )
    others = call(
        lambda *refs: cross_kernel(axes, *refs),
        f32(INL, CRS, NT),
        held,
        merged,
        other,
        cells_v,
        cells_c,
        timed,
        scratch=((2 * RUN, ROWS, LANES), (cells, LANES)),
    )
    return call(
        finish_kernel, f32(INL, CRS, NT), volume, cond, ends.reshape(WIDE * 4, LANES), others
    )


def solution(mesh):
    axes = ("wide", "narrow")
    return jax.shard_map(
        lambda volume: per_device(axes, volume),
        mesh=mesh,
        in_specs=(P("wide", "narrow", None),),
        out_specs=P("wide", "narrow", None),
        check_vma=False,
    )
```

```python
import jax
import jax.numpy as jnp
from jax import lax
from jax.experimental import pallas as pl
from jax.experimental.pallas import tpu as pltpu
from jax.sharding import PartitionSpec as P

half_weight = 150.0
contrast_sq = 9.0

WIDE = 64
NARROW = 8
INL = 4
CRS = 16
NT = 1024
LANES = 128
TILES = NT // LANES
ROWS = INL * TILES
GROUP = 8
PORTS = 7
RUN = 4


def condense(mass, rhs, link):
    mass, rhs, right = list(mass), list(rhs), list(link)
    alive, steps = list(range(len(mass))), []
    while len(alive) > 2:
        gone = set()
        for at in range(1, len(alive) - 1, 2):
            l, k, r = alive[at - 1 : at + 2]
            inverse = 1.0 / (right[l] + right[k] + mass[k])
            to_left, to_right = right[l] * inverse, right[k] * inverse
            mass[l] = mass[l] + to_left * mass[k]
            rhs[l] = rhs[l] + to_left * rhs[k]
            mass[r] = mass[r] + to_right * mass[k]
            rhs[r] = rhs[r] + to_right * rhs[k]
            right[l] = to_left * right[k]
            steps.append((l, k, r, to_left, to_right, rhs[k] * inverse))
            gone.add(k)
        alive = [k for k in alive if k not in gone]
    return mass[0], rhs[0], mass[-1], rhs[-1], right[0], steps


def expand(first, last, steps, count):
    x = [None] * count
    x[0], x[-1] = first, last
    for l, k, r, to_left, to_right, base in reversed(steps):
        x[k] = base + to_left * x[l] + to_right * x[r]
    return x


def links(cond):
    return [half_weight * (a + b) for a, b in zip(cond[:-1], cond[1:])]


def halving(mass, rhs, before, after, shift, count):
    step = 1
    while step < count:
        inverse = 1.0 / (before + after + mass)
        to_left, to_right = before * inverse, after * inverse
        across = to_left * after
        mass, rhs = (
            mass + shift(to_right * mass, step) + shift(to_left * mass, -step),
            rhs + shift(to_right * rhs, step) + shift(to_left * rhs, -step),
        )
        before, after = shift(across, step), shift(across, -step)
        step *= 2
    return rhs / mass


def iota(shape, dim):
    return lax.broadcasted_iota(jnp.int32, shape, dim)


def lane_tile(t):
    return slice(t * LANES, (t + 1) * LANES)


def prepare_kernel(
    axes, vol, wide0, wide1, narrow0, narrow1, cond, wide_out, narrow_out, cells_v, cells_c
):
    wide_axes, narrow_axes = axes
    wide_rank, narrow_rank = lax.axis_index(wide_axes), lax.axis_index(narrow_axes)
    wide_even, narrow_even = lax.rem(wide_rank, 2) == 0, lax.rem(narrow_rank, 2) == 0
    col = iota((CRS, NT), 1)
    row = iota((CRS, NT), 0)
    for i in range(INL):
        here = vol[i]
        if i == 0:
            up = jnp.where(wide_even, wide1[0], wide0[0])
            up = jnp.where(wide_rank == 0, here, up)
        else:
            up = vol[i - 1]
        if i == INL - 1:
            down = jnp.where(wide_even, wide0[0], wide1[0])
            down = jnp.where(wide_rank == WIDE - 1, here, down)
        else:
            down = vol[i + 1]
        power = (0.5 * (down - up)) ** 2
        edge = jnp.where(narrow_even, narrow1[i], narrow0[i])
        edge = jnp.where(narrow_rank == 0, here[:1], edge)
        lower = jnp.where(row == 0, edge, pltpu.roll(here, 1, 0))
        edge = jnp.where(narrow_even, narrow0[i], narrow1[i])
        edge = jnp.where(narrow_rank == NARROW - 1, here[CRS - 1 :], edge)
        upper = jnp.where(row == CRS - 1, edge, pltpu.roll(here, CRS - 1, 0))
        power = power + (0.5 * (upper - lower)) ** 2
        earlier = jnp.where(col == 0, here, pltpu.roll(here, 1, 1))
        later = jnp.where(col == NT - 1, here, pltpu.roll(here, NT - 1, 1))
        power = power + (0.5 * (later - earlier)) ** 2
        value = contrast_sq / (contrast_sq + power)
        cond[i] = value
        for t in range(TILES):
            where = pl.ds(i * TILES + t, CRS, stride=ROWS)
            cells_v[where, :] = here[:, lane_tile(t)]
            cells_c[where, :] = value[:, lane_tile(t)]
    ones = jnp.ones((ROWS, LANES), jnp.float32)
    v = [cells_v[pl.ds(c * ROWS, ROWS), :] for c in range(CRS)]
    k = [cells_c[pl.ds(c * ROWS, ROWS), :] for c in range(CRS)]
    m0, d0, m1, d1, g, _ = condense([ones] * CRS, v, links(k))
    for p, value in enumerate((g, m0, m1, d0, d1, k[0], k[-1])):
        narrow_out[p * ROWS : (p + 1) * ROWS, :] = value
    ones = jnp.ones((GROUP, LANES), jnp.float32)
    for t in range(TILES):
        for u in range(CRS // GROUP):
            at = (slice(u * GROUP, (u + 1) * GROUP), lane_tile(t))
            v = [vol[(i, *at)] for i in range(INL)]
            k = [cond[(i, *at)] for i in range(INL)]
            m0, d0, m1, d1, g, _ = condense([ones] * INL, v, links(k))
            for p, value in enumerate((g, m0, m1, d0, d1, k[0], k[-1])):
                start = t * GROUP * 2 * PORTS + p * 2 + u
                wide_out[pl.ds(start, GROUP, stride=2 * PORTS), :] = value


def sublane_shift(x, s):
    return pltpu.roll(x, s % GROUP, 0)


def wide_kernel(ports, out):
    part = WIDE // GROUP
    sub = iota((GROUP, LANES), 0)
    zero = jnp.zeros((GROUP, LANES), jnp.float32)
    for u in range(2):

        def port(p, j):
            return ports[pl.ds(j * 2 * PORTS + p * 2 + u, GROUP, stride=part * 2 * PORTS), :]

        last_cond = sublane_shift(port(6, part - 1), 1)
        mass, rhs, link = [zero], [zero], []
        for j in range(part):
            joined = half_weight * (last_cond + port(5, j))
            if j == 0:
                joined = jnp.where(sub == 0, 0.0, joined)
            link += [joined, port(0, j)]
            mass += [port(1, j), port(2, j)]
            rhs += [port(3, j), port(4, j)]
            last_cond = port(6, j)
        count = len(mass)
        m0, d0, m1, d1, g, steps = condense(mass, rhs, link)
        last = halving(
            m1 + sublane_shift(m0, -1),
            d1 + sublane_shift(d0, -1),
            g,
            sublane_shift(g, -1),
            sublane_shift,
            GROUP,
        )
        x = expand(sublane_shift(last, 1), last, steps, count)
        for j in range(part):
            for e in range(2):
                out[pl.ds(j * 4 + e * 2 + u, GROUP, stride=part * 4), :] = x[1 + 2 * j + e]


def time_kernel(vol, cond, out, cells_v, cells_c, link_s, tmp):
    lines = INL * CRS
    half = NT // 2
    blocks = half // LANES
    for b in range(blocks):
        for source, cells in ((vol, cells_v), (cond, cells_c)):
            stacked = jnp.concatenate(
                [
                    source[:, :, b * LANES : (b + 1) * LANES].reshape(lines, LANES),
                    source[:, :, half + b * LANES : half + (b + 1) * LANES].reshape(lines, LANES),
                ],
                0,
            )
            cells[b * LANES : (b + 1) * LANES, :] = stacked.T
    lane = iota((GROUP, LANES), 1)
    sub = iota((GROUP, LANES), 0)
    low = lane < lines

    def swap(x):
        return pltpu.roll(x, lines, 1)

    for s in range(half // GROUP):
        here = cells_c[s * GROUP : (s + 1) * GROUP, :]
        if s:
            edge = cells_c[s * GROUP - 1 : s * GROUP, :]
        else:
            edge = swap(cells_c[half - GROUP : half, :])[GROUP - 1 :]
        value = half_weight * (here + jnp.where(sub == 0, edge, pltpu.roll(here, 1, 0)))
        if s == 0:
            value = jnp.where((sub == 0) & low, 0.0, value)
        link_s[s * GROUP : (s + 1) * GROUP, :] = value

    def chain_shift(x, s):
        n = x.shape[0]
        if abs(s) == n:
            return swap(x)
        rolled = pltpu.roll(x, s % n, 0)
        place = iota(x.shape, 0)
        wrapped = place < s if s > 0 else place >= n + s
        return jnp.where(wrapped, swap(rolled), rolled)

    runs = half // GROUP
    zero = jnp.zeros((runs, LANES), jnp.float32)
    ones = jnp.ones((runs, LANES), jnp.float32)
    v = [cells_v[pl.ds(k, runs, stride=GROUP), :] for k in range(GROUP)]
    link = [link_s[pl.ds(k, runs, stride=GROUP), :] for k in range(GROUP)]
    m0, d0, m1, d1, g, steps = condense([zero] + [ones] * GROUP, [zero] + v, link)
    tmp[0] = m1 + chain_shift(m0, -1)
    tmp[1] = d1 + chain_shift(d0, -1)
    tmp[2] = g
    zero = jnp.zeros((GROUP, LANES), jnp.float32)

    def take(p):
        return [tmp[p, pl.ds(k, GROUP, stride=GROUP), :] for k in range(GROUP)]

    m0, d0, m1, d1, g, inner = condense([zero] + take(0), [zero] + take(1), take(2))
    last = halving(
        m1 + chain_shift(m0, -1),
        d1 + chain_shift(d0, -1),
        g,
        chain_shift(g, -1),
        chain_shift,
        2 * GROUP,
    )
    x = expand(chain_shift(last, 1), last, inner, GROUP + 1)
    for k in range(GROUP):
        tmp[0, pl.ds(k, GROUP, stride=GROUP), :] = x[k + 1]
    last = tmp[0]
    x = expand(chain_shift(last, 1), last, steps, GROUP + 1)
    for k in range(GROUP):
        cells_v[pl.ds(k, runs, stride=GROUP), :] = x[k + 1]
    for b in range(blocks):
        turned = cells_v[b * LANES : (b + 1) * LANES, :].T
        for h in range(2):
            out[:, :, h * half + b * LANES : h * half + (b + 1) * LANES] = turned[
                h * lines : (h + 1) * lines
            ].reshape(INL, CRS, LANES)


def ports_of(ref):
    return [ref[p * ROWS : (p + 1) * ROWS, :] for p in range(PORTS)]


def chain_of(ports):
    mass, rhs, link = [], [], []
    for n, (g, m0, m1, d0, d1, _, _) in enumerate(ports):
        mass += [m0, m1]
        rhs += [d0, d1]
        link.append(g)
        if n < len(ports) - 1:
            link.append(half_weight * (ports[n][6] + ports[n + 1][5]))
    return mass, rhs, link


def merge_kernel(axes, own, by1, by2, by3, held, merged):
    place = lax.rem(lax.axis_index(axes[1]), RUN)
    for step, ref in enumerate((own, by1, by2, by3)):
        held[place ^ step] = ref[...]
    _, edge = facing(held, lax.axis_index(axes[1]) >= RUN)
    for p, value in enumerate(edge):
        merged[p * ROWS : (p + 1) * ROWS, :] = value


def facing(held, high):
    ports = [ports_of(held.at[n]) for n in range(RUN)]
    m0, d0, m1, d1, g, steps = condense(*chain_of(ports))
    here_m, here_d = jnp.where(high, m0, m1), jnp.where(high, d0, d1)
    away_m, away_d = jnp.where(high, m1, m0), jnp.where(high, d1, d0)
    inverse = 1.0 / (g + away_m)
    slope, base = g * inverse, away_d * inverse
    edge = (here_m + slope * away_m, here_d + slope * away_d, jnp.where(high, ports[0][5], ports[-1][6]))
    return (slope, base, steps), edge


def cross_kernel(axes, held, other, cells_v, cells_c, timed, out, ends, cells_x):
    rank = lax.axis_index(axes[1])
    place, high = lax.rem(rank, RUN), rank >= RUN
    (slope, base, steps), (m0, d0, c0) = facing(held, high)
    m1, d1, c1 = [other[p * ROWS : (p + 1) * ROWS, :] for p in range(3)]
    link = half_weight * (c0 + c1)
    here = (d0 * (m1 + link) + link * d1) / (m0 * m1 + link * (m0 + m1))
    away = base + slope * here
    first, last = jnp.where(high, here, away), jnp.where(high, away, here)
    for n, value in enumerate(expand(first, last, steps, 2 * RUN)):
        ends[n] = value
    v = [cells_v[pl.ds(c * ROWS, ROWS), :] for c in range(CRS)]
    k = [cells_c[pl.ds(c * ROWS, ROWS), :] for c in range(CRS)]
    ones = jnp.ones((ROWS, LANES), jnp.float32)
    steps = condense([ones] * CRS, v, links(k))[-1]
    x = expand(ends[2 * place], ends[2 * place + 1], steps, CRS)
    for c in range(CRS):
        cells_x[c * ROWS : (c + 1) * ROWS, :] = x[c]
    for i in range(INL):
        for t in range(TILES):
            out[i, :, lane_tile(t)] = (
                timed[i, :, lane_tile(t)] + cells_x[pl.ds(i * TILES + t, CRS, stride=ROWS), :]
            )


def finish_kernel(vol, cond, ends, others, out):
    ones = jnp.ones((GROUP, LANES), jnp.float32)
    for t in range(TILES):
        for u in range(CRS // GROUP):
            at = (slice(u * GROUP, (u + 1) * GROUP), lane_tile(t))
            v = [vol[(i, *at)] for i in range(INL)]
            k = [cond[(i, *at)] for i in range(INL)]
            steps = condense([ones] * INL, v, links(k))[-1]
            first = ends[pl.ds(t * GROUP * 4 + u, GROUP, stride=4), :]
            last = ends[pl.ds(t * GROUP * 4 + 2 + u, GROUP, stride=4), :]
            for i, x in enumerate(expand(first, last, steps, INL)):
                out[(i, *at)] = (x + others[(i, *at)]) * (1.0 / 3.0)


def f32(*shape):
    return jax.ShapeDtypeStruct(shape, jnp.float32)


def call(kernel, out, *args, scratch=()):
    return pl.pallas_call(
        kernel,
        out_shape=out,
        scratch_shapes=[pltpu.VMEM(s, jnp.float32) for s in scratch],
        compiler_params=pltpu.CompilerParams(vmem_limit_bytes=16 * 2**20),
    )(*args)


def per_device(axes, volume):
    wide_axes, narrow_axes = axes

    def exchanged(dim, axis, count):
        odd = lax.rem(lax.axis_index(axis), 2)
        end = volume.shape[dim] - 1
        got = []
        for start in range(2):
            pairs = [(i, i + 1) for i in range(start, count - 1, 2)]
            at = end * (odd ^ 1 ^ start)
            layer = lax.dynamic_slice_in_dim(volume, at, 1, dim)
            got.append(lax.ppermute(layer, axis, pairs + [(j, i) for i, j in pairs]))
        return got

    cells = CRS * ROWS
    cond, wide_ports, narrow_ports, cells_v, cells_c = call(
        lambda *refs: prepare_kernel(axes, *refs),
        (
            f32(INL, CRS, NT),
            f32(WIDE * PORTS * 2, LANES),
            f32(PORTS * ROWS, LANES),
            f32(cells, LANES),
            f32(cells, LANES),
        ),
        volume,
        *exchanged(0, wide_axes, WIDE),
        *exchanged(1, narrow_axes, NARROW),
    )
    lines = lax.all_to_all(
        wide_ports.reshape(WIDE, PORTS, 2, LANES), wide_axes, split_axis=0, concat_axis=0, tiled=True
    )

    def swapped(x, step):
        return lax.ppermute(x, narrow_axes, [(n, n ^ step) for n in range(NARROW)])

    held, merged = call(
        lambda *refs: merge_kernel(axes, *refs),
        (f32(RUN, PORTS * ROWS, LANES), f32(3 * ROWS, LANES)),
        narrow_ports,
        *[swapped(narrow_ports, step) for step in range(1, RUN)],
    )
    other = swapped(merged, RUN)
    timed = call(
        time_kernel,
        f32(INL, CRS, NT),
        volume,
        cond,
        scratch=(
            (NT // 2, LANES),
            (NT // 2, LANES),
            (NT // 2, LANES),
            (3, NT // 2 // GROUP, LANES),
        ),
    )
    lines, held, timed = lax.optimization_barrier((lines, held, timed))
    solved = call(
        wide_kernel, f32(WIDE * 4, LANES), lines.reshape(WIDE * PORTS * 2, LANES)
    )
    ends = lax.all_to_all(
        solved.reshape(WIDE, 2, 2, LANES), wide_axes, split_axis=0, concat_axis=0, tiled=True
    )
    others = call(
        lambda *refs: cross_kernel(axes, *refs),
        f32(INL, CRS, NT),
        held,
        other,
        cells_v,
        cells_c,
        timed,
        scratch=((2 * RUN, ROWS, LANES), (cells, LANES)),
    )
    return call(
        finish_kernel, f32(INL, CRS, NT), volume, cond, ends.reshape(WIDE * 4, LANES), others
    )


def solution(mesh):
    axes = ("wide", "narrow")
    return jax.shard_map(
        lambda volume: per_device(axes, volume),
        mesh=mesh,
        in_specs=(P("wide", "narrow", None),),
        out_specs=P("wide", "narrow", None),
        check_vma=False,
    )
```

```python
import jax
import jax.numpy as jnp
from jax import lax
from jax.experimental import pallas as pl
from jax.experimental.pallas import tpu as pltpu
from jax.sharding import PartitionSpec as P

half_weight = 150.0
contrast_sq = 9.0

WIDE = 64
NARROW = 8
INL = 4
CRS = 16
NT = 1024
LANES = 128
TILES = NT // LANES
ROWS = INL * TILES
GROUP = 8
PORTS = 7
RUN = 4


def condense(mass, rhs, link):
    mass, rhs, right = list(mass), list(rhs), list(link)
    alive, steps = list(range(len(mass))), []
    while len(alive) > 2:
        gone = set()
        for at in range(1, len(alive) - 1, 2):
            l, k, r = alive[at - 1 : at + 2]
            inverse = 1.0 / (right[l] + right[k] + mass[k])
            to_left, to_right = right[l] * inverse, right[k] * inverse
            mass[l] = mass[l] + to_left * mass[k]
            rhs[l] = rhs[l] + to_left * rhs[k]
            mass[r] = mass[r] + to_right * mass[k]
            rhs[r] = rhs[r] + to_right * rhs[k]
            right[l] = to_left * right[k]
            steps.append((l, k, r, to_left, to_right, rhs[k] * inverse))
            gone.add(k)
        alive = [k for k in alive if k not in gone]
    return mass[0], rhs[0], mass[-1], rhs[-1], right[0], steps


def expand(first, last, steps, count):
    x = [None] * count
    x[0], x[-1] = first, last
    for l, k, r, to_left, to_right, base in reversed(steps):
        x[k] = base + to_left * x[l] + to_right * x[r]
    return x


def links(cond):
    return [half_weight * (a + b) for a, b in zip(cond[:-1], cond[1:])]


def halving(mass, rhs, before, after, shift, count):
    step = 1
    while step < count:
        inverse = 1.0 / (before + after + mass)
        to_left, to_right = before * inverse, after * inverse
        across = to_left * after
        mass, rhs = (
            mass + shift(to_right * mass, step) + shift(to_left * mass, -step),
            rhs + shift(to_right * rhs, step) + shift(to_left * rhs, -step),
        )
        before, after = shift(across, step), shift(across, -step)
        step *= 2
    return rhs / mass


def iota(shape, dim):
    return lax.broadcasted_iota(jnp.int32, shape, dim)


def lane_tile(t):
    return slice(t * LANES, (t + 1) * LANES)


def faces_kernel(axes, vol, narrow1, wide1, narrow0, wide0):
    wide_even, narrow_even = [lax.rem(lax.axis_index(axis), 2) == 0 for axis in axes]
    first, last = vol[0], vol[INL - 1]
    wide1[0] = jnp.where(wide_even, first, last)
    wide0[0] = jnp.where(wide_even, last, first)
    for i in range(INL):
        first, last = vol[i, :1], vol[i, CRS - 1 :]
        narrow1[i] = jnp.where(narrow_even, first, last)
        narrow0[i] = jnp.where(narrow_even, last, first)


def prepare_kernel(
    axes, vol, narrow1, wide1, narrow0, wide0, cond, wide_out, narrow_out, cells_v, cells_c
):
    wide_axes, narrow_axes = axes
    wide_rank, narrow_rank = lax.axis_index(wide_axes), lax.axis_index(narrow_axes)
    wide_even, narrow_even = lax.rem(wide_rank, 2) == 0, lax.rem(narrow_rank, 2) == 0
    col = iota((CRS, NT), 1)
    row = iota((CRS, NT), 0)
    for i in range(INL):
        here = vol[i]
        if i == 0:
            up = jnp.where(wide_even, wide1[0], wide0[0])
            up = jnp.where(wide_rank == 0, here, up)
        else:
            up = vol[i - 1]
        if i == INL - 1:
            down = jnp.where(wide_even, wide0[0], wide1[0])
            down = jnp.where(wide_rank == WIDE - 1, here, down)
        else:
            down = vol[i + 1]
        power = (0.5 * (down - up)) ** 2
        edge = jnp.where(narrow_even, narrow1[i], narrow0[i])
        edge = jnp.where(narrow_rank == 0, here[:1], edge)
        lower = jnp.where(row == 0, edge, pltpu.roll(here, 1, 0))
        edge = jnp.where(narrow_even, narrow0[i], narrow1[i])
        edge = jnp.where(narrow_rank == NARROW - 1, here[CRS - 1 :], edge)
        upper = jnp.where(row == CRS - 1, edge, pltpu.roll(here, CRS - 1, 0))
        power = power + (0.5 * (upper - lower)) ** 2
        earlier = jnp.where(col == 0, here, pltpu.roll(here, 1, 1))
        later = jnp.where(col == NT - 1, here, pltpu.roll(here, NT - 1, 1))
        power = power + (0.5 * (later - earlier)) ** 2
        value = contrast_sq / (contrast_sq + power)
        cond[i] = value
        for t in range(TILES):
            where = pl.ds(i * TILES + t, CRS, stride=ROWS)
            cells_v[where, :] = here[:, lane_tile(t)]
            cells_c[where, :] = value[:, lane_tile(t)]
    ones = jnp.ones((ROWS, LANES), jnp.float32)
    v = [cells_v[pl.ds(c * ROWS, ROWS), :] for c in range(CRS)]
    k = [cells_c[pl.ds(c * ROWS, ROWS), :] for c in range(CRS)]
    m0, d0, m1, d1, g, _ = condense([ones] * CRS, v, links(k))
    for p, value in enumerate((g, m0, m1, d0, d1, k[0], k[-1])):
        narrow_out[p * ROWS : (p + 1) * ROWS, :] = value
    ones = jnp.ones((GROUP, LANES), jnp.float32)
    for t in range(TILES):
        for u in range(CRS // GROUP):
            at = (slice(u * GROUP, (u + 1) * GROUP), lane_tile(t))
            v = [vol[(i, *at)] for i in range(INL)]
            k = [cond[(i, *at)] for i in range(INL)]
            m0, d0, m1, d1, g, _ = condense([ones] * INL, v, links(k))
            for p, value in enumerate((g, m0, m1, d0, d1, k[0], k[-1])):
                start = t * GROUP * 2 * PORTS + p * 2 + u
                wide_out[pl.ds(start, GROUP, stride=2 * PORTS), :] = value


def sublane_shift(x, s):
    return pltpu.roll(x, s % GROUP, 0)


def wide_kernel(ports, out):
    part = WIDE // GROUP
    sub = iota((GROUP, LANES), 0)
    zero = jnp.zeros((GROUP, LANES), jnp.float32)
    for u in range(2):

        def port(p, j):
            return ports[pl.ds(j * 2 * PORTS + p * 2 + u, GROUP, stride=part * 2 * PORTS), :]

        last_cond = sublane_shift(port(6, part - 1), 1)
        mass, rhs, link = [zero], [zero], []
        for j in range(part):
            joined = half_weight * (last_cond + port(5, j))
            if j == 0:
                joined = jnp.where(sub == 0, 0.0, joined)
            link += [joined, port(0, j)]
            mass += [port(1, j), port(2, j)]
            rhs += [port(3, j), port(4, j)]
            last_cond = port(6, j)
        count = len(mass)
        m0, d0, m1, d1, g, steps = condense(mass, rhs, link)
        last = halving(
            m1 + sublane_shift(m0, -1),
            d1 + sublane_shift(d0, -1),
            g,
            sublane_shift(g, -1),
            sublane_shift,
            GROUP,
        )
        x = expand(sublane_shift(last, 1), last, steps, count)
        for j in range(part):
            for e in range(2):
                out[pl.ds(j * 4 + e * 2 + u, GROUP, stride=part * 4), :] = x[1 + 2 * j + e]


def time_kernel(vol, cond, out, cells_v, cells_c, link_s, tmp):
    lines = INL * CRS
    half = NT // 2
    blocks = half // LANES
    for b in range(blocks):
        for source, cells in ((vol, cells_v), (cond, cells_c)):
            stacked = jnp.concatenate(
                [
                    source[:, :, b * LANES : (b + 1) * LANES].reshape(lines, LANES),
                    source[:, :, half + b * LANES : half + (b + 1) * LANES].reshape(lines, LANES),
                ],
                0,
            )
            cells[b * LANES : (b + 1) * LANES, :] = stacked.T
    lane = iota((GROUP, LANES), 1)
    sub = iota((GROUP, LANES), 0)
    low = lane < lines

    def swap(x):
        return pltpu.roll(x, lines, 1)

    for s in range(half // GROUP):
        here = cells_c[s * GROUP : (s + 1) * GROUP, :]
        if s:
            edge = cells_c[s * GROUP - 1 : s * GROUP, :]
        else:
            edge = swap(cells_c[half - GROUP : half, :])[GROUP - 1 :]
        value = half_weight * (here + jnp.where(sub == 0, edge, pltpu.roll(here, 1, 0)))
        if s == 0:
            value = jnp.where((sub == 0) & low, 0.0, value)
        link_s[s * GROUP : (s + 1) * GROUP, :] = value

    def chain_shift(x, s):
        n = x.shape[0]
        if abs(s) == n:
            return swap(x)
        rolled = pltpu.roll(x, s % n, 0)
        place = iota(x.shape, 0)
        wrapped = place < s if s > 0 else place >= n + s
        return jnp.where(wrapped, swap(rolled), rolled)

    runs = half // GROUP
    zero = jnp.zeros((runs, LANES), jnp.float32)
    ones = jnp.ones((runs, LANES), jnp.float32)
    v = [cells_v[pl.ds(k, runs, stride=GROUP), :] for k in range(GROUP)]
    link = [link_s[pl.ds(k, runs, stride=GROUP), :] for k in range(GROUP)]
    m0, d0, m1, d1, g, steps = condense([zero] + [ones] * GROUP, [zero] + v, link)
    tmp[0] = m1 + chain_shift(m0, -1)
    tmp[1] = d1 + chain_shift(d0, -1)
    tmp[2] = g
    zero = jnp.zeros((GROUP, LANES), jnp.float32)

    def take(p):
        return [tmp[p, pl.ds(k, GROUP, stride=GROUP), :] for k in range(GROUP)]

    m0, d0, m1, d1, g, inner = condense([zero] + take(0), [zero] + take(1), take(2))
    last = halving(
        m1 + chain_shift(m0, -1),
        d1 + chain_shift(d0, -1),
        g,
        chain_shift(g, -1),
        chain_shift,
        2 * GROUP,
    )
    x = expand(chain_shift(last, 1), last, inner, GROUP + 1)
    for k in range(GROUP):
        tmp[0, pl.ds(k, GROUP, stride=GROUP), :] = x[k + 1]
    last = tmp[0]
    x = expand(chain_shift(last, 1), last, steps, GROUP + 1)
    for k in range(GROUP):
        cells_v[pl.ds(k, runs, stride=GROUP), :] = x[k + 1]
    for b in range(blocks):
        turned = cells_v[b * LANES : (b + 1) * LANES, :].T
        for h in range(2):
            out[:, :, h * half + b * LANES : h * half + (b + 1) * LANES] = turned[
                h * lines : (h + 1) * lines
            ].reshape(INL, CRS, LANES)


def ports_of(ref):
    return [ref[p * ROWS : (p + 1) * ROWS, :] for p in range(PORTS)]


def chain_of(ports):
    mass, rhs, link = [], [], []
    for n, (g, m0, m1, d0, d1, _, _) in enumerate(ports):
        mass += [m0, m1]
        rhs += [d0, d1]
        link.append(g)
        if n < len(ports) - 1:
            link.append(half_weight * (ports[n][6] + ports[n + 1][5]))
    return mass, rhs, link


def merge_kernel(axes, own, by2, by1, by3, held, merged):
    place = lax.rem(lax.axis_index(axes[1]), RUN)
    for step, ref in enumerate((own, by1, by2, by3)):
        held[place ^ step] = ref[...]
    _, edge = facing(held, lax.axis_index(axes[1]) >= RUN)
    for p, value in enumerate(edge):
        merged[p * ROWS : (p + 1) * ROWS, :] = value


def facing(held, high):
    ports = [ports_of(held.at[n]) for n in range(RUN)]
    m0, d0, m1, d1, g, steps = condense(*chain_of(ports))
    here_m, here_d = jnp.where(high, m0, m1), jnp.where(high, d0, d1)
    away_m, away_d = jnp.where(high, m1, m0), jnp.where(high, d1, d0)
    inverse = 1.0 / (g + away_m)
    slope, base = g * inverse, away_d * inverse
    edge = (here_m + slope * away_m, here_d + slope * away_d, jnp.where(high, ports[0][5], ports[-1][6]))
    return (slope, base, steps), edge


def cross_kernel(axes, held, other, cells_v, cells_c, timed, out, ends, cells_x):
    rank = lax.axis_index(axes[1])
    place, high = lax.rem(rank, RUN), rank >= RUN
    (slope, base, steps), (m0, d0, c0) = facing(held, high)
    m1, d1, c1 = [other[p * ROWS : (p + 1) * ROWS, :] for p in range(3)]
    link = half_weight * (c0 + c1)
    here = (d0 * (m1 + link) + link * d1) / (m0 * m1 + link * (m0 + m1))
    away = base + slope * here
    first, last = jnp.where(high, here, away), jnp.where(high, away, here)
    for n, value in enumerate(expand(first, last, steps, 2 * RUN)):
        ends[n] = value
    v = [cells_v[pl.ds(c * ROWS, ROWS), :] for c in range(CRS)]
    k = [cells_c[pl.ds(c * ROWS, ROWS), :] for c in range(CRS)]
    ones = jnp.ones((ROWS, LANES), jnp.float32)
    steps = condense([ones] * CRS, v, links(k))[-1]
    x = expand(ends[2 * place], ends[2 * place + 1], steps, CRS)
    for c in range(CRS):
        cells_x[c * ROWS : (c + 1) * ROWS, :] = x[c]
    for i in range(INL):
        for t in range(TILES):
            out[i, :, lane_tile(t)] = (
                timed[i, :, lane_tile(t)] + cells_x[pl.ds(i * TILES + t, CRS, stride=ROWS), :]
            )


def finish_kernel(vol, cond, ends, others, out):
    ones = jnp.ones((GROUP, LANES), jnp.float32)
    for t in range(TILES):
        for u in range(CRS // GROUP):
            at = (slice(u * GROUP, (u + 1) * GROUP), lane_tile(t))
            v = [vol[(i, *at)] for i in range(INL)]
            k = [cond[(i, *at)] for i in range(INL)]
            steps = condense([ones] * INL, v, links(k))[-1]
            first = ends[pl.ds(t * GROUP * 4 + u, GROUP, stride=4), :]
            last = ends[pl.ds(t * GROUP * 4 + 2 + u, GROUP, stride=4), :]
            for i, x in enumerate(expand(first, last, steps, INL)):
                out[(i, *at)] = (x + others[(i, *at)]) * (1.0 / 3.0)


def f32(*shape):
    return jax.ShapeDtypeStruct(shape, jnp.float32)


def call(kernel, out, *args, scratch=()):
    return pl.pallas_call(
        kernel,
        out_shape=out,
        scratch_shapes=[pltpu.VMEM(s, jnp.float32) for s in scratch],
        compiler_params=pltpu.CompilerParams(vmem_limit_bytes=16 * 2**20),
    )(*args)


def per_device(axes, volume):
    wide_axes, narrow_axes = axes

    def exchanged(layer, axis, count, start):
        pairs = [(i, i + 1) for i in range(start, count - 1, 2)]
        return lax.ppermute(layer, axis, pairs + [(j, i) for i, j in pairs])

    inline_face, cross_face = f32(1, CRS, NT), f32(INL, 1, NT)
    narrow1, wide1, narrow0, wide0 = call(
        lambda *refs: faces_kernel(axes, *refs),
        (cross_face, inline_face, cross_face, inline_face),
        volume,
    )
    narrow1 = exchanged(narrow1, narrow_axes, NARROW, 1)
    wide1 = exchanged(wide1, wide_axes, WIDE, 1)
    narrow0 = exchanged(narrow0, narrow_axes, NARROW, 0)
    wide0 = exchanged(wide0, wide_axes, WIDE, 0)
    cells = CRS * ROWS
    cond, wide_ports, narrow_ports, cells_v, cells_c = call(
        lambda *refs: prepare_kernel(axes, *refs),
        (
            f32(INL, CRS, NT),
            f32(WIDE * PORTS * 2, LANES),
            f32(PORTS * ROWS, LANES),
            f32(cells, LANES),
            f32(cells, LANES),
        ),
        volume,
        narrow1,
        wide1,
        narrow0,
        wide0,
    )
    lines = lax.all_to_all(
        wide_ports.reshape(WIDE, PORTS, 2, LANES), wide_axes, split_axis=0, concat_axis=0, tiled=True
    )

    def swapped(x, step):
        return lax.ppermute(x, narrow_axes, [(n, n ^ step) for n in range(NARROW)])

    held, merged = call(
        lambda *refs: merge_kernel(axes, *refs),
        (f32(RUN, PORTS * ROWS, LANES), f32(3 * ROWS, LANES)),
        narrow_ports,
        *[swapped(narrow_ports, step) for step in (2, 1, 3)],
    )
    other = swapped(merged, RUN)
    timed = call(
        time_kernel,
        f32(INL, CRS, NT),
        volume,
        cond,
        scratch=(
            (NT // 2, LANES),
            (NT // 2, LANES),
            (NT // 2, LANES),
            (3, NT // 2 // GROUP, LANES),
        ),
    )
    lines, held, timed, other = lax.optimization_barrier((lines, held, timed, other))
    solved = call(
        wide_kernel, f32(WIDE * 4, LANES), lines.reshape(WIDE * PORTS * 2, LANES)
    )
    ends = lax.all_to_all(
        solved.reshape(WIDE, 2, 2, LANES), wide_axes, split_axis=0, concat_axis=0, tiled=True
    )
    others = call(
        lambda *refs: cross_kernel(axes, *refs),
        f32(INL, CRS, NT),
        held,
        other,
        cells_v,
        cells_c,
        timed,
        scratch=((2 * RUN, ROWS, LANES), (cells, LANES)),
    )
    return call(
        finish_kernel, f32(INL, CRS, NT), volume, cond, ends.reshape(WIDE * 4, LANES), others
    )


def solution(mesh):
    axes = ("wide", "narrow")
    return jax.shard_map(
        lambda volume: per_device(axes, volume),
        mesh=mesh,
        in_specs=(P("wide", "narrow", None),),
        out_specs=P("wide", "narrow", None),
        check_vma=False,
    )
```

```python
import jax
import jax.numpy as jnp
from jax import lax
from jax.experimental import pallas as pl
from jax.experimental.pallas import tpu as pltpu
from jax.sharding import PartitionSpec as P

half_weight = 150.0
contrast_sq = 9.0

WIDE = 64
NARROW = 8
INL = 4
CRS = 16
NT = 1024
LANES = 128
TILES = NT // LANES
ROWS = INL * TILES
GROUP = 8
PORTS = 7
WPORTS = INL + 2
RUN = 4


def condense(mass, rhs, link):
    mass, rhs, right = list(mass), list(rhs), list(link)
    alive, steps = list(range(len(mass))), []
    while len(alive) > 2:
        gone = set()
        for at in range(1, len(alive) - 1, 2):
            l, k, r = alive[at - 1 : at + 2]
            inverse = 1.0 / (right[l] + right[k] + mass[k])
            to_left, to_right = right[l] * inverse, right[k] * inverse
            mass[l] = mass[l] + to_left * mass[k]
            rhs[l] = rhs[l] + to_left * rhs[k]
            mass[r] = mass[r] + to_right * mass[k]
            rhs[r] = rhs[r] + to_right * rhs[k]
            right[l] = to_left * right[k]
            steps.append((l, k, r, to_left, to_right, rhs[k] * inverse))
            gone.add(k)
        alive = [k for k in alive if k not in gone]
    return mass[0], rhs[0], mass[-1], rhs[-1], right[0], steps


def expand(first, last, steps, count):
    x = [None] * count
    x[0], x[-1] = first, last
    for l, k, r, to_left, to_right, base in reversed(steps):
        x[k] = base + to_left * x[l] + to_right * x[r]
    return x


def links(cond):
    return [half_weight * (a + b) for a, b in zip(cond[:-1], cond[1:])]


def halving(mass, rhs, before, after, shift, count):
    step = 1
    while step < count:
        inverse = 1.0 / (before + after + mass)
        to_left, to_right = before * inverse, after * inverse
        across = to_left * after
        mass, rhs = (
            mass + shift(to_right * mass, step) + shift(to_left * mass, -step),
            rhs + shift(to_right * rhs, step) + shift(to_left * rhs, -step),
        )
        before, after = shift(across, step), shift(across, -step)
        step *= 2
    return rhs / mass


def iota(shape, dim):
    return lax.broadcasted_iota(jnp.int32, shape, dim)


def lane_tile(t):
    return slice(t * LANES, (t + 1) * LANES)


def faces_kernel(axes, vol, narrow1, wide1, narrow0, wide0):
    wide_even, narrow_even = [lax.rem(lax.axis_index(axis), 2) == 0 for axis in axes]
    first, last = vol[0], vol[INL - 1]
    wide1[0] = jnp.where(wide_even, first, last)
    wide0[0] = jnp.where(wide_even, last, first)
    for i in range(INL):
        first, last = vol[i, :1], vol[i, CRS - 1 :]
        narrow1[i] = jnp.where(narrow_even, first, last)
        narrow0[i] = jnp.where(narrow_even, last, first)


def prepare_kernel(
    axes, vol, narrow1, wide1, narrow0, wide0, cond, wide_out, narrow_out, cells_v, cells_c
):
    wide_axes, narrow_axes = axes
    wide_rank, narrow_rank = lax.axis_index(wide_axes), lax.axis_index(narrow_axes)
    wide_even, narrow_even = lax.rem(wide_rank, 2) == 0, lax.rem(narrow_rank, 2) == 0
    col = iota((CRS, NT), 1)
    row = iota((CRS, NT), 0)
    for i in range(INL):
        here = vol[i]
        if i == 0:
            up = jnp.where(wide_even, wide1[0], wide0[0])
            up = jnp.where(wide_rank == 0, here, up)
        else:
            up = vol[i - 1]
        if i == INL - 1:
            down = jnp.where(wide_even, wide0[0], wide1[0])
            down = jnp.where(wide_rank == WIDE - 1, here, down)
        else:
            down = vol[i + 1]
        power = (0.5 * (down - up)) ** 2
        edge = jnp.where(narrow_even, narrow1[i], narrow0[i])
        edge = jnp.where(narrow_rank == 0, here[:1], edge)
        lower = jnp.where(row == 0, edge, pltpu.roll(here, 1, 0))
        edge = jnp.where(narrow_even, narrow0[i], narrow1[i])
        edge = jnp.where(narrow_rank == NARROW - 1, here[CRS - 1 :], edge)
        upper = jnp.where(row == CRS - 1, edge, pltpu.roll(here, CRS - 1, 0))
        power = power + (0.5 * (upper - lower)) ** 2
        earlier = jnp.where(col == 0, here, pltpu.roll(here, 1, 1))
        later = jnp.where(col == NT - 1, here, pltpu.roll(here, NT - 1, 1))
        power = power + (0.5 * (later - earlier)) ** 2
        value = contrast_sq / (contrast_sq + power)
        cond[i] = value
        for t in range(TILES):
            where = pl.ds(i * TILES + t, CRS, stride=ROWS)
            cells_v[where, :] = here[:, lane_tile(t)]
            cells_c[where, :] = value[:, lane_tile(t)]
    ones = jnp.ones((ROWS, LANES), jnp.float32)
    v = [cells_v[pl.ds(c * ROWS, ROWS), :] for c in range(CRS)]
    k = [cells_c[pl.ds(c * ROWS, ROWS), :] for c in range(CRS)]
    m0, d0, m1, d1, g, _ = condense([ones] * CRS, v, links(k))
    for p, value in enumerate((g, m0, m1, d0, d1, k[0], k[-1])):
        narrow_out[p * ROWS : (p + 1) * ROWS, :] = value
    ones = jnp.ones((GROUP, LANES), jnp.float32)
    for t in range(TILES):
        for u in range(CRS // GROUP):
            at = (slice(u * GROUP, (u + 1) * GROUP), lane_tile(t))
            v = [vol[(i, *at)] for i in range(INL)]
            k = [cond[(i, *at)] for i in range(INL)]
            _, d0, _, d1, _, _ = condense([ones] * INL, v, links(k))
            for p, value in enumerate((*k, d0, d1)):
                start = t * GROUP * 2 * WPORTS + p * 2 + u
                wide_out[pl.ds(start, GROUP, stride=2 * WPORTS), :] = value


def sublane_shift(x, s):
    return pltpu.roll(x, s % GROUP, 0)


def wide_kernel(ports, out):
    part = WIDE // GROUP
    sub = iota((GROUP, LANES), 0)
    zero = jnp.zeros((GROUP, LANES), jnp.float32)
    ones = jnp.ones((GROUP, LANES), jnp.float32)
    for u in range(2):

        def port(p, j):
            return ports[pl.ds(j * 2 * WPORTS + p * 2 + u, GROUP, stride=part * 2 * WPORTS), :]

        last_cond = sublane_shift(port(INL - 1, part - 1), 1)
        mass, rhs, link = [zero], [zero], []
        for j in range(part):
            k = [port(p, j) for p in range(INL)]
            joined = half_weight * (last_cond + k[0])
            if j == 0:
                joined = jnp.where(sub == 0, 0.0, joined)
            m0, _, m1, _, g, _ = condense([ones] * INL, [zero] * INL, links(k))
            link += [joined, g]
            mass += [m0, m1]
            rhs += [port(INL, j), port(INL + 1, j)]
            last_cond = k[-1]
        count = len(mass)
        m0, d0, m1, d1, g, steps = condense(mass, rhs, link)
        last = halving(
            m1 + sublane_shift(m0, -1),
            d1 + sublane_shift(d0, -1),
            g,
            sublane_shift(g, -1),
            sublane_shift,
            GROUP,
        )
        x = expand(sublane_shift(last, 1), last, steps, count)
        for j in range(part):
            for e in range(2):
                out[pl.ds(j * 4 + e * 2 + u, GROUP, stride=part * 4), :] = x[1 + 2 * j + e]


def time_kernel(vol, cond, out, cells_v, cells_c, link_s, tmp):
    lines = INL * CRS
    half = NT // 2
    blocks = half // LANES
    for b in range(blocks):
        for source, cells in ((vol, cells_v), (cond, cells_c)):
            stacked = jnp.concatenate(
                [
                    source[:, :, b * LANES : (b + 1) * LANES].reshape(lines, LANES),
                    source[:, :, half + b * LANES : half + (b + 1) * LANES].reshape(lines, LANES),
                ],
                0,
            )
            cells[b * LANES : (b + 1) * LANES, :] = stacked.T
    lane = iota((GROUP, LANES), 1)
    sub = iota((GROUP, LANES), 0)
    low = lane < lines

    def swap(x):
        return pltpu.roll(x, lines, 1)

    for s in range(half // GROUP):
        here = cells_c[s * GROUP : (s + 1) * GROUP, :]
        if s:
            edge = cells_c[s * GROUP - 1 : s * GROUP, :]
        else:
            edge = swap(cells_c[half - GROUP : half, :])[GROUP - 1 :]
        value = half_weight * (here + jnp.where(sub == 0, edge, pltpu.roll(here, 1, 0)))
        if s == 0:
            value = jnp.where((sub == 0) & low, 0.0, value)
        link_s[s * GROUP : (s + 1) * GROUP, :] = value

    def chain_shift(x, s):
        n = x.shape[0]
        if abs(s) == n:
            return swap(x)
        rolled = pltpu.roll(x, s % n, 0)
        place = iota(x.shape, 0)
        wrapped = place < s if s > 0 else place >= n + s
        return jnp.where(wrapped, swap(rolled), rolled)

    runs = half // GROUP
    zero = jnp.zeros((runs, LANES), jnp.float32)
    ones = jnp.ones((runs, LANES), jnp.float32)
    v = [cells_v[pl.ds(k, runs, stride=GROUP), :] for k in range(GROUP)]
    link = [link_s[pl.ds(k, runs, stride=GROUP), :] for k in range(GROUP)]
    m0, d0, m1, d1, g, steps = condense([zero] + [ones] * GROUP, [zero] + v, link)
    tmp[0] = m1 + chain_shift(m0, -1)
    tmp[1] = d1 + chain_shift(d0, -1)
    tmp[2] = g
    zero = jnp.zeros((GROUP, LANES), jnp.float32)

    def take(p):
        return [tmp[p, pl.ds(k, GROUP, stride=GROUP), :] for k in range(GROUP)]

    m0, d0, m1, d1, g, inner = condense([zero] + take(0), [zero] + take(1), take(2))
    last = halving(
        m1 + chain_shift(m0, -1),
        d1 + chain_shift(d0, -1),
        g,
        chain_shift(g, -1),
        chain_shift,
        2 * GROUP,
    )
    x = expand(chain_shift(last, 1), last, inner, GROUP + 1)
    for k in range(GROUP):
        tmp[0, pl.ds(k, GROUP, stride=GROUP), :] = x[k + 1]
    last = tmp[0]
    x = expand(chain_shift(last, 1), last, steps, GROUP + 1)
    for k in range(GROUP):
        cells_v[pl.ds(k, runs, stride=GROUP), :] = x[k + 1]
    for b in range(blocks):
        turned = cells_v[b * LANES : (b + 1) * LANES, :].T
        for h in range(2):
            out[:, :, h * half + b * LANES : h * half + (b + 1) * LANES] = turned[
                h * lines : (h + 1) * lines
            ].reshape(INL, CRS, LANES)


def ports_of(ref):
    return [ref[p * ROWS : (p + 1) * ROWS, :] for p in range(PORTS)]


def chain_of(ports):
    mass, rhs, link = [], [], []
    for n, (g, m0, m1, d0, d1, _, _) in enumerate(ports):
        mass += [m0, m1]
        rhs += [d0, d1]
        link.append(g)
        if n < len(ports) - 1:
            link.append(half_weight * (ports[n][6] + ports[n + 1][5]))
    return mass, rhs, link


def in_order(mine, theirs, first):
    return [
        [jnp.where(first, a, b) for a, b in zip(mine, theirs)],
        [jnp.where(first, b, a) for a, b in zip(mine, theirs)],
    ]


def places(axes):
    rank = lax.axis_index(axes[1])
    return lax.rem(rank, 2) == 0, lax.rem(rank, RUN) < 2, rank < RUN


def join_kernel(axes, own, beside, joined):
    pair = in_order(ports_of(own), ports_of(beside), places(axes)[0])
    m0, d0, m1, d1, g, _ = condense(*chain_of(pair))
    for p, value in enumerate((g, m0, m1, d0, d1, pair[0][5], pair[1][6])):
        joined[p * ROWS : (p + 1) * ROWS, :] = value


def facing(run, low):
    m0, d0, m1, d1, g, steps = condense(*chain_of(run))
    here_m, here_d = jnp.where(low, m1, m0), jnp.where(low, d1, d0)
    away_m, away_d = jnp.where(low, m0, m1), jnp.where(low, d0, d1)
    inverse = 1.0 / (g + away_m)
    slope, base = g * inverse, away_d * inverse
    edge = (here_m + slope * away_m, here_d + slope * away_d, jnp.where(low, run[-1][6], run[0][5]))
    return (slope, base, steps), edge


def edge_kernel(axes, joined, across, out):
    _, second, low = places(axes)
    _, edge = facing(in_order(ports_of(joined), ports_of(across), second), low)
    for p, value in enumerate(edge):
        out[p * ROWS : (p + 1) * ROWS, :] = value


def half_of(x, first):
    return jnp.where(first, x[0], x[2]), jnp.where(first, x[1], x[3])


def cross_kernel(
    axes, own, beside, joined, across, other, cells_v, cells_c, timed, out, cells_x
):
    first, second, low = places(axes)
    run = in_order(ports_of(joined), ports_of(across), second)
    (slope, base, steps), (m0, d0, c0) = facing(run, low)
    m1, d1, c1 = [other[p * ROWS : (p + 1) * ROWS, :] for p in range(3)]
    link = half_weight * (c0 + c1)
    here = (d0 * (m1 + link) + link * d1) / (m0 * m1 + link * (m0 + m1))
    away = base + slope * here
    x = expand(jnp.where(low, away, here), jnp.where(low, here, away), steps, 4)
    steps = condense(*chain_of(in_order(ports_of(own), ports_of(beside), first)))[-1]
    x = expand(*half_of(x, second), steps, 4)
    v = [cells_v[pl.ds(c * ROWS, ROWS), :] for c in range(CRS)]
    k = [cells_c[pl.ds(c * ROWS, ROWS), :] for c in range(CRS)]
    ones = jnp.ones((ROWS, LANES), jnp.float32)
    steps = condense([ones] * CRS, v, links(k))[-1]
    x = expand(*half_of(x, first), steps, CRS)
    for c in range(CRS):
        cells_x[c * ROWS : (c + 1) * ROWS, :] = x[c]
    for i in range(INL):
        for t in range(TILES):
            out[i, :, lane_tile(t)] = (
                timed[i, :, lane_tile(t)] + cells_x[pl.ds(i * TILES + t, CRS, stride=ROWS), :]
            )


def finish_kernel(vol, cond, ends, others, out):
    ones = jnp.ones((GROUP, LANES), jnp.float32)
    for t in range(TILES):
        for u in range(CRS // GROUP):
            at = (slice(u * GROUP, (u + 1) * GROUP), lane_tile(t))
            v = [vol[(i, *at)] for i in range(INL)]
            k = [cond[(i, *at)] for i in range(INL)]
            steps = condense([ones] * INL, v, links(k))[-1]
            first = ends[pl.ds(t * GROUP * 4 + u, GROUP, stride=4), :]
            last = ends[pl.ds(t * GROUP * 4 + 2 + u, GROUP, stride=4), :]
            for i, x in enumerate(expand(first, last, steps, INL)):
                out[(i, *at)] = (x + others[(i, *at)]) * (1.0 / 3.0)


def f32(*shape):
    return jax.ShapeDtypeStruct(shape, jnp.float32)


def call(kernel, out, *args, scratch=()):
    return pl.pallas_call(
        kernel,
        out_shape=out,
        scratch_shapes=[pltpu.VMEM(s, jnp.float32) for s in scratch],
        compiler_params=pltpu.CompilerParams(vmem_limit_bytes=16 * 2**20),
    )(*args)


def per_device(axes, volume):
    wide_axes, narrow_axes = axes

    def exchanged(layer, axis, count, start):
        pairs = [(i, i + 1) for i in range(start, count - 1, 2)]
        return lax.ppermute(layer, axis, pairs + [(j, i) for i, j in pairs])

    inline_face, cross_face = f32(1, CRS, NT), f32(INL, 1, NT)
    narrow1, wide1, narrow0, wide0 = call(
        lambda *refs: faces_kernel(axes, *refs),
        (cross_face, inline_face, cross_face, inline_face),
        volume,
    )
    narrow1 = exchanged(narrow1, narrow_axes, NARROW, 1)
    wide1 = exchanged(wide1, wide_axes, WIDE, 1)
    narrow0 = exchanged(narrow0, narrow_axes, NARROW, 0)
    wide0 = exchanged(wide0, wide_axes, WIDE, 0)
    cells = CRS * ROWS
    cond, wide_ports, narrow_ports, cells_v, cells_c = call(
        lambda *refs: prepare_kernel(axes, *refs),
        (
            f32(INL, CRS, NT),
            f32(WIDE * WPORTS * 2, LANES),
            f32(PORTS * ROWS, LANES),
            f32(cells, LANES),
            f32(cells, LANES),
        ),
        volume,
        narrow1,
        wide1,
        narrow0,
        wide0,
    )
    lines = lax.all_to_all(
        wide_ports.reshape(WIDE, WPORTS, 2, LANES), wide_axes, split_axis=0, concat_axis=0, tiled=True
    )

    def swapped(x, step):
        return lax.ppermute(x, narrow_axes, [(n, n ^ step) for n in range(NARROW)])

    beside = swapped(narrow_ports, 1)
    joined = call(
        lambda *refs: join_kernel(axes, *refs), f32(PORTS * ROWS, LANES), narrow_ports, beside
    )
    across = swapped(joined, 2)
    edge = call(lambda *refs: edge_kernel(axes, *refs), f32(3 * ROWS, LANES), joined, across)
    other = swapped(edge, RUN)
    timed = call(
        time_kernel,
        f32(INL, CRS, NT),
        volume,
        cond,
        scratch=(
            (NT // 2, LANES),
            (NT // 2, LANES),
            (NT // 2, LANES),
            (3, NT // 2 // GROUP, LANES),
        ),
    )
    lines, edge, timed = lax.optimization_barrier((lines, edge, timed))
    solved = call(
        wide_kernel, f32(WIDE * 4, LANES), lines.reshape(WIDE * WPORTS * 2, LANES)
    )
    ends = lax.all_to_all(
        solved.reshape(WIDE, 2, 2, LANES), wide_axes, split_axis=0, concat_axis=0, tiled=True
    )
    others = call(
        lambda *refs: cross_kernel(axes, *refs),
        f32(INL, CRS, NT),
        narrow_ports,
        beside,
        joined,
        across,
        other,
        cells_v,
        cells_c,
        timed,
        scratch=((cells, LANES),),
    )
    return call(
        finish_kernel, f32(INL, CRS, NT), volume, cond, ends.reshape(WIDE * 4, LANES), others
    )


def solution(mesh):
    axes = ("wide", "narrow")
    return jax.shard_map(
        lambda volume: per_device(axes, volume),
        mesh=mesh,
        in_specs=(P("wide", "narrow", None),),
        out_specs=P("wide", "narrow", None),
        check_vma=False,
    )
```

```python
import jax
import jax.numpy as jnp
from jax import lax
from jax.experimental import pallas as pl
from jax.experimental.pallas import tpu as pltpu
from jax.sharding import PartitionSpec as P

half_weight = 150.0
contrast_sq = 9.0

WIDE = 64
NARROW = 8
INL = 4
CRS = 16
NT = 1024
LANES = 128
TILES = NT // LANES
ROWS = INL * TILES
GROUP = 8
PORTS = 7
WPORTS = INL + 2
RUN = 4


def condense(mass, rhs, link):
    mass, rhs, right = list(mass), list(rhs), list(link)
    alive, steps = list(range(len(mass))), []
    while len(alive) > 2:
        gone = set()
        for at in range(1, len(alive) - 1, 2):
            l, k, r = alive[at - 1 : at + 2]
            inverse = 1.0 / (right[l] + right[k] + mass[k])
            to_left, to_right = right[l] * inverse, right[k] * inverse
            mass[l] = mass[l] + to_left * mass[k]
            rhs[l] = rhs[l] + to_left * rhs[k]
            mass[r] = mass[r] + to_right * mass[k]
            rhs[r] = rhs[r] + to_right * rhs[k]
            right[l] = to_left * right[k]
            steps.append((l, k, r, to_left, to_right, rhs[k] * inverse))
            gone.add(k)
        alive = [k for k in alive if k not in gone]
    return mass[0], rhs[0], mass[-1], rhs[-1], right[0], steps


def expand(first, last, steps, count):
    x = [None] * count
    x[0], x[-1] = first, last
    for l, k, r, to_left, to_right, base in reversed(steps):
        x[k] = base + to_left * x[l] + to_right * x[r]
    return x


def links(cond):
    return [half_weight * (a + b) for a, b in zip(cond[:-1], cond[1:])]


def halving(mass, rhs, before, after, shift, count):
    step = 1
    while step < count:
        inverse = 1.0 / (before + after + mass)
        to_left, to_right = before * inverse, after * inverse
        across = to_left * after
        mass, rhs = (
            mass + shift(to_right * mass, step) + shift(to_left * mass, -step),
            rhs + shift(to_right * rhs, step) + shift(to_left * rhs, -step),
        )
        before, after = shift(across, step), shift(across, -step)
        step *= 2
    return rhs / mass


def iota(shape, dim):
    return lax.broadcasted_iota(jnp.int32, shape, dim)


def lane_tile(t):
    return slice(t * LANES, (t + 1) * LANES)


def faces_kernel(axes, vol, narrow1, wide1, narrow0, wide0):
    wide_even, narrow_even = [lax.rem(lax.axis_index(axis), 2) == 0 for axis in axes]
    first, last = vol[0], vol[INL - 1]
    wide1[0] = jnp.where(wide_even, first, last)
    wide0[0] = jnp.where(wide_even, last, first)
    for i in range(INL):
        first, last = vol[i, :1], vol[i, CRS - 1 :]
        narrow1[i] = jnp.where(narrow_even, first, last)
        narrow0[i] = jnp.where(narrow_even, last, first)
    for ref in (narrow1, narrow0):
        ref[INL:] = jnp.zeros((CRS + 1 - INL, 1, NT), jnp.float32)


def prepare_kernel(
    axes, vol, narrow1, wide1, narrow0, wide0, cond, wide_out, narrow_out, cells_v, cells_c
):
    wide_axes, narrow_axes = axes
    wide_rank, narrow_rank = lax.axis_index(wide_axes), lax.axis_index(narrow_axes)
    wide_even, narrow_even = lax.rem(wide_rank, 2) == 0, lax.rem(narrow_rank, 2) == 0
    col = iota((CRS, NT), 1)
    row = iota((CRS, NT), 0)
    for i in range(INL):
        here = vol[i]
        if i == 0:
            up = jnp.where(wide_even, wide1[0], wide0[0])
            up = jnp.where(wide_rank == 0, here, up)
        else:
            up = vol[i - 1]
        if i == INL - 1:
            down = jnp.where(wide_even, wide0[0], wide1[0])
            down = jnp.where(wide_rank == WIDE - 1, here, down)
        else:
            down = vol[i + 1]
        power = (0.5 * (down - up)) ** 2
        edge = jnp.where(narrow_even, narrow1[i], narrow0[i])
        edge = jnp.where(narrow_rank == 0, here[:1], edge)
        lower = jnp.where(row == 0, edge, pltpu.roll(here, 1, 0))
        edge = jnp.where(narrow_even, narrow0[i], narrow1[i])
        edge = jnp.where(narrow_rank == NARROW - 1, here[CRS - 1 :], edge)
        upper = jnp.where(row == CRS - 1, edge, pltpu.roll(here, CRS - 1, 0))
        power = power + (0.5 * (upper - lower)) ** 2
        earlier = jnp.where(col == 0, here, pltpu.roll(here, 1, 1))
        later = jnp.where(col == NT - 1, here, pltpu.roll(here, NT - 1, 1))
        power = power + (0.5 * (later - earlier)) ** 2
        value = contrast_sq / (contrast_sq + power)
        cond[i] = value
        for t in range(TILES):
            where = pl.ds(i * TILES + t, CRS, stride=ROWS)
            cells_v[where, :] = here[:, lane_tile(t)]
            cells_c[where, :] = value[:, lane_tile(t)]
    ones = jnp.ones((ROWS, LANES), jnp.float32)
    v = [cells_v[pl.ds(c * ROWS, ROWS), :] for c in range(CRS)]
    k = [cells_c[pl.ds(c * ROWS, ROWS), :] for c in range(CRS)]
    m0, d0, m1, d1, g, _ = condense([ones] * CRS, v, links(k))
    for p, value in enumerate((g, m0, m1, d0, d1, k[0], k[-1])):
        narrow_out[p * ROWS : (p + 1) * ROWS, :] = value
    ones = jnp.ones((GROUP, LANES), jnp.float32)
    for t in range(TILES):
        for u in range(CRS // GROUP):
            at = (slice(u * GROUP, (u + 1) * GROUP), lane_tile(t))
            v = [vol[(i, *at)] for i in range(INL)]
            k = [cond[(i, *at)] for i in range(INL)]
            _, d0, _, d1, _, _ = condense([ones] * INL, v, links(k))
            for p, value in enumerate((*k, d0, d1)):
                start = t * GROUP * 2 * WPORTS + p * 2 + u
                wide_out[pl.ds(start, GROUP, stride=2 * WPORTS), :] = value


def sublane_shift(x, s):
    return pltpu.roll(x, s % GROUP, 0)


def wide_kernel(ports, out):
    part = WIDE // GROUP
    sub = iota((GROUP, LANES), 0)
    zero = jnp.zeros((GROUP, LANES), jnp.float32)
    ones = jnp.ones((GROUP, LANES), jnp.float32)
    for u in range(2):

        def port(p, j):
            return ports[pl.ds(j * 2 * WPORTS + p * 2 + u, GROUP, stride=part * 2 * WPORTS), :]

        last_cond = sublane_shift(port(INL - 1, part - 1), 1)
        mass, rhs, link = [zero], [zero], []
        for j in range(part):
            k = [port(p, j) for p in range(INL)]
            joined = half_weight * (last_cond + k[0])
            if j == 0:
                joined = jnp.where(sub == 0, 0.0, joined)
            m0, _, m1, _, g, _ = condense([ones] * INL, [zero] * INL, links(k))
            link += [joined, g]
            mass += [m0, m1]
            rhs += [port(INL, j), port(INL + 1, j)]
            last_cond = k[-1]
        count = len(mass)
        m0, d0, m1, d1, g, steps = condense(mass, rhs, link)
        last = halving(
            m1 + sublane_shift(m0, -1),
            d1 + sublane_shift(d0, -1),
            g,
            sublane_shift(g, -1),
            sublane_shift,
            GROUP,
        )
        x = expand(sublane_shift(last, 1), last, steps, count)
        for j in range(part):
            for e in range(2):
                out[pl.ds(j * 4 + e * 2 + u, GROUP, stride=part * 4), :] = x[1 + 2 * j + e]


def time_kernel(vol, cond, out, cells_v, cells_c, link_s, tmp):
    lines = INL * CRS
    half = NT // 2
    blocks = half // LANES
    for b in range(blocks):
        for source, cells in ((vol, cells_v), (cond, cells_c)):
            stacked = jnp.concatenate(
                [
                    source[:, :, b * LANES : (b + 1) * LANES].reshape(lines, LANES),
                    source[:, :, half + b * LANES : half + (b + 1) * LANES].reshape(lines, LANES),
                ],
                0,
            )
            cells[b * LANES : (b + 1) * LANES, :] = stacked.T
    lane = iota((GROUP, LANES), 1)
    sub = iota((GROUP, LANES), 0)
    low = lane < lines

    def swap(x):
        return pltpu.roll(x, lines, 1)

    for s in range(half // GROUP):
        here = cells_c[s * GROUP : (s + 1) * GROUP, :]
        if s:
            edge = cells_c[s * GROUP - 1 : s * GROUP, :]
        else:
            edge = swap(cells_c[half - GROUP : half, :])[GROUP - 1 :]
        value = half_weight * (here + jnp.where(sub == 0, edge, pltpu.roll(here, 1, 0)))
        if s == 0:
            value = jnp.where((sub == 0) & low, 0.0, value)
        link_s[s * GROUP : (s + 1) * GROUP, :] = value

    def chain_shift(x, s):
        n = x.shape[0]
        if abs(s) == n:
            return swap(x)
        rolled = pltpu.roll(x, s % n, 0)
        place = iota(x.shape, 0)
        wrapped = place < s if s > 0 else place >= n + s
        return jnp.where(wrapped, swap(rolled), rolled)

    runs = half // GROUP
    zero = jnp.zeros((runs, LANES), jnp.float32)
    ones = jnp.ones((runs, LANES), jnp.float32)
    v = [cells_v[pl.ds(k, runs, stride=GROUP), :] for k in range(GROUP)]
    link = [link_s[pl.ds(k, runs, stride=GROUP), :] for k in range(GROUP)]
    m0, d0, m1, d1, g, steps = condense([zero] + [ones] * GROUP, [zero] + v, link)
    tmp[0] = m1 + chain_shift(m0, -1)
    tmp[1] = d1 + chain_shift(d0, -1)
    tmp[2] = g
    zero = jnp.zeros((GROUP, LANES), jnp.float32)

    def take(p):
        return [tmp[p, pl.ds(k, GROUP, stride=GROUP), :] for k in range(GROUP)]

    m0, d0, m1, d1, g, inner = condense([zero] + take(0), [zero] + take(1), take(2))
    last = halving(
        m1 + chain_shift(m0, -1),
        d1 + chain_shift(d0, -1),
        g,
        chain_shift(g, -1),
        chain_shift,
        2 * GROUP,
    )
    x = expand(chain_shift(last, 1), last, inner, GROUP + 1)
    for k in range(GROUP):
        tmp[0, pl.ds(k, GROUP, stride=GROUP), :] = x[k + 1]
    last = tmp[0]
    x = expand(chain_shift(last, 1), last, steps, GROUP + 1)
    for k in range(GROUP):
        cells_v[pl.ds(k, runs, stride=GROUP), :] = x[k + 1]
    for b in range(blocks):
        turned = cells_v[b * LANES : (b + 1) * LANES, :].T
        for h in range(2):
            out[:, :, h * half + b * LANES : h * half + (b + 1) * LANES] = turned[
                h * lines : (h + 1) * lines
            ].reshape(INL, CRS, LANES)


def ports_of(ref):
    return [ref[p * ROWS : (p + 1) * ROWS, :] for p in range(PORTS)]


def chain_of(ports):
    mass, rhs, link = [], [], []
    for n, (g, m0, m1, d0, d1, _, _) in enumerate(ports):
        mass += [m0, m1]
        rhs += [d0, d1]
        link.append(g)
        if n < len(ports) - 1:
            link.append(half_weight * (ports[n][6] + ports[n + 1][5]))
    return mass, rhs, link


def in_order(mine, theirs, first):
    return [
        [jnp.where(first, a, b) for a, b in zip(mine, theirs)],
        [jnp.where(first, b, a) for a, b in zip(mine, theirs)],
    ]


def places(axes):
    rank = lax.axis_index(axes[1])
    return lax.rem(rank, 2) == 0, lax.rem(rank, RUN) < 2, rank < RUN


def join_kernel(axes, own, beside, joined):
    pair = in_order(ports_of(own), ports_of(beside), places(axes)[0])
    m0, d0, m1, d1, g, _ = condense(*chain_of(pair))
    for p, value in enumerate((g, m0, m1, d0, d1, pair[0][5], pair[1][6])):
        joined[p * ROWS : (p + 1) * ROWS, :] = value


def facing(run, low):
    m0, d0, m1, d1, g, steps = condense(*chain_of(run))
    here_m, here_d = jnp.where(low, m1, m0), jnp.where(low, d1, d0)
    away_m, away_d = jnp.where(low, m0, m1), jnp.where(low, d0, d1)
    inverse = 1.0 / (g + away_m)
    slope, base = g * inverse, away_d * inverse
    edge = (here_m + slope * away_m, here_d + slope * away_d, jnp.where(low, run[-1][6], run[0][5]))
    return (slope, base, steps), edge


def edge_kernel(axes, joined, across, out):
    _, second, low = places(axes)
    _, edge = facing(in_order(ports_of(joined), ports_of(across), second), low)
    for p, value in enumerate(edge):
        out[p * ROWS : (p + 1) * ROWS, :] = value


def half_of(x, first):
    return jnp.where(first, x[0], x[2]), jnp.where(first, x[1], x[3])


def cross_kernel(
    axes, own, beside, joined, across, other, cells_v, cells_c, timed, out, cells_x
):
    first, second, low = places(axes)
    run = in_order(ports_of(joined), ports_of(across), second)
    (slope, base, steps), (m0, d0, c0) = facing(run, low)
    m1, d1, c1 = [other[p * ROWS : (p + 1) * ROWS, :] for p in range(3)]
    link = half_weight * (c0 + c1)
    here = (d0 * (m1 + link) + link * d1) / (m0 * m1 + link * (m0 + m1))
    away = base + slope * here
    x = expand(jnp.where(low, away, here), jnp.where(low, here, away), steps, 4)
    steps = condense(*chain_of(in_order(ports_of(own), ports_of(beside), first)))[-1]
    x = expand(*half_of(x, second), steps, 4)
    v = [cells_v[pl.ds(c * ROWS, ROWS), :] for c in range(CRS)]
    k = [cells_c[pl.ds(c * ROWS, ROWS), :] for c in range(CRS)]
    ones = jnp.ones((ROWS, LANES), jnp.float32)
    steps = condense([ones] * CRS, v, links(k))[-1]
    x = expand(*half_of(x, first), steps, CRS)
    for c in range(CRS):
        cells_x[c * ROWS : (c + 1) * ROWS, :] = x[c]
    for i in range(INL):
        for t in range(TILES):
            out[i, :, lane_tile(t)] = (
                timed[i, :, lane_tile(t)] + cells_x[pl.ds(i * TILES + t, CRS, stride=ROWS), :]
            )


def finish_kernel(vol, cond, ends, others, out):
    ones = jnp.ones((GROUP, LANES), jnp.float32)
    for t in range(TILES):
        for u in range(CRS // GROUP):
            at = (slice(u * GROUP, (u + 1) * GROUP), lane_tile(t))
            v = [vol[(i, *at)] for i in range(INL)]
            k = [cond[(i, *at)] for i in range(INL)]
            steps = condense([ones] * INL, v, links(k))[-1]
            first = ends[pl.ds(t * GROUP * 4 + u, GROUP, stride=4), :]
            last = ends[pl.ds(t * GROUP * 4 + 2 + u, GROUP, stride=4), :]
            for i, x in enumerate(expand(first, last, steps, INL)):
                out[(i, *at)] = (x + others[(i, *at)]) * (1.0 / 3.0)


def f32(*shape):
    return jax.ShapeDtypeStruct(shape, jnp.float32)


def call(kernel, out, *args, scratch=()):
    return pl.pallas_call(
        kernel,
        out_shape=out,
        scratch_shapes=[pltpu.VMEM(s, jnp.float32) for s in scratch],
        compiler_params=pltpu.CompilerParams(vmem_limit_bytes=16 * 2**20),
    )(*args)


def per_device(axes, volume):
    wide_axes, narrow_axes = axes

    def exchanged(layer, axis, count, start):
        pairs = [(i, i + 1) for i in range(start, count - 1, 2)]
        return lax.ppermute(layer, axis, pairs + [(j, i) for i, j in pairs])

    inline_face, longer = f32(1, CRS, NT), f32(CRS + 1, 1, NT)
    narrow1, wide1, narrow0, wide0 = call(
        lambda *refs: faces_kernel(axes, *refs),
        (longer, inline_face, longer, inline_face),
        volume,
    )
    narrow1 = exchanged(narrow1, narrow_axes, NARROW, 1)
    wide1 = exchanged(wide1, wide_axes, WIDE, 1)
    narrow0 = exchanged(narrow0, narrow_axes, NARROW, 0)
    wide0 = exchanged(wide0, wide_axes, WIDE, 0)
    cells = CRS * ROWS
    cond, wide_ports, narrow_ports, cells_v, cells_c = call(
        lambda *refs: prepare_kernel(axes, *refs),
        (
            f32(INL, CRS, NT),
            f32(WIDE * WPORTS * 2, LANES),
            f32(PORTS * ROWS, LANES),
            f32(cells, LANES),
            f32(cells, LANES),
        ),
        volume,
        narrow1,
        wide1,
        narrow0,
        wide0,
    )
    lines = lax.all_to_all(
        wide_ports.reshape(WIDE, WPORTS, 2, LANES), wide_axes, split_axis=0, concat_axis=0, tiled=True
    )

    def swapped(x, step):
        return lax.ppermute(x, narrow_axes, [(n, n ^ step) for n in range(NARROW)])

    beside = swapped(narrow_ports, 1)
    joined = call(
        lambda *refs: join_kernel(axes, *refs), f32(PORTS * ROWS, LANES), narrow_ports, beside
    )
    across = swapped(joined, 3)
    edge = call(lambda *refs: edge_kernel(axes, *refs), f32(3 * ROWS, LANES), joined, across)
    other = swapped(edge, RUN)
    timed = call(
        time_kernel,
        f32(INL, CRS, NT),
        volume,
        cond,
        scratch=(
            (NT // 2, LANES),
            (NT // 2, LANES),
            (NT // 2, LANES),
            (3, NT // 2 // GROUP, LANES),
        ),
    )
    lines, edge = lax.optimization_barrier((lines, edge))
    solved = call(
        wide_kernel, f32(WIDE * 4, LANES), lines.reshape(WIDE * WPORTS * 2, LANES)
    )
    ends = lax.all_to_all(
        solved.reshape(WIDE, 2, 2, LANES), wide_axes, split_axis=0, concat_axis=0, tiled=True
    )
    others = call(
        lambda *refs: cross_kernel(axes, *refs),
        f32(INL, CRS, NT),
        narrow_ports,
        beside,
        joined,
        across,
        other,
        cells_v,
        cells_c,
        timed,
        scratch=((cells, LANES),),
    )
    return call(
        finish_kernel, f32(INL, CRS, NT), volume, cond, ends.reshape(WIDE * 4, LANES), others
    )


def solution(mesh):
    axes = ("wide", "narrow")
    return jax.shard_map(
        lambda volume: per_device(axes, volume),
        mesh=mesh,
        in_specs=(P("wide", "narrow", None),),
        out_specs=P("wide", "narrow", None),
        check_vma=False,
    )
```

```python
import jax
import jax.numpy as jnp
from jax import lax
from jax.experimental import pallas as pl
from jax.experimental.pallas import tpu as pltpu
from jax.sharding import PartitionSpec as P

half_weight = 150.0
contrast_sq = 9.0

WIDE = 64
NARROW = 8
INL = 4
CRS = 16
NT = 1024
LANES = 128
TILES = NT // LANES
ROWS = INL * TILES
GROUP = 8
PORTS = 7
WPORTS = INL + 2
RUN = 4


def condense(mass, rhs, link):
    mass, rhs, right = list(mass), list(rhs), list(link)
    alive, steps = list(range(len(mass))), []
    while len(alive) > 2:
        gone = set()
        for at in range(1, len(alive) - 1, 2):
            l, k, r = alive[at - 1 : at + 2]
            inverse = 1.0 / (right[l] + right[k] + mass[k])
            to_left, to_right = right[l] * inverse, right[k] * inverse
            mass[l] = mass[l] + to_left * mass[k]
            rhs[l] = rhs[l] + to_left * rhs[k]
            mass[r] = mass[r] + to_right * mass[k]
            rhs[r] = rhs[r] + to_right * rhs[k]
            right[l] = to_left * right[k]
            steps.append((l, k, r, to_left, to_right, rhs[k] * inverse))
            gone.add(k)
        alive = [k for k in alive if k not in gone]
    return mass[0], rhs[0], mass[-1], rhs[-1], right[0], steps


def expand(first, last, steps, count):
    x = [None] * count
    x[0], x[-1] = first, last
    for l, k, r, to_left, to_right, base in reversed(steps):
        x[k] = base + to_left * x[l] + to_right * x[r]
    return x


def links(cond):
    return [half_weight * (a + b) for a, b in zip(cond[:-1], cond[1:])]


def halving(mass, rhs, before, after, shift, count):
    step = 1
    while step < count:
        inverse = 1.0 / (before + after + mass)
        to_left, to_right = before * inverse, after * inverse
        across = to_left * after
        mass, rhs = (
            mass + shift(to_right * mass, step) + shift(to_left * mass, -step),
            rhs + shift(to_right * rhs, step) + shift(to_left * rhs, -step),
        )
        before, after = shift(across, step), shift(across, -step)
        step *= 2
    return rhs / mass


def iota(shape, dim):
    return lax.broadcasted_iota(jnp.int32, shape, dim)


def lane_tile(t):
    return slice(t * LANES, (t + 1) * LANES)


def faces_kernel(axes, vol, narrow1, wide1, narrow0, wide0):
    wide_even, narrow_even = [lax.rem(lax.axis_index(axis), 2) == 0 for axis in axes]
    first, last = vol[0], vol[INL - 1]
    wide1[0] = jnp.where(wide_even, first, last)
    wide0[0] = jnp.where(wide_even, last, first)
    for i in range(INL):
        first, last = vol[i, :1], vol[i, CRS - 1 :]
        narrow1[i] = jnp.where(narrow_even, first, last)
        narrow0[i] = jnp.where(narrow_even, last, first)
    for ref in (narrow1, narrow0):
        ref[INL:] = jnp.zeros((CRS + 1 - INL, 1, NT), jnp.float32)


def conductivity(power):
    return contrast_sq / (contrast_sq + power)


def partial_kernel(axes, vol, narrow1, narrow0, partial, cells_v):
    rank = lax.axis_index(axes[1])
    even = lax.rem(rank, 2) == 0
    col = iota((CRS, NT), 1)
    row = iota((CRS, NT), 0)
    for i in range(INL):
        here = vol[i]
        edge = jnp.where(even, narrow1[i], narrow0[i])
        edge = jnp.where(rank == 0, here[:1], edge)
        lower = jnp.where(row == 0, edge, pltpu.roll(here, 1, 0))
        edge = jnp.where(even, narrow0[i], narrow1[i])
        edge = jnp.where(rank == NARROW - 1, here[CRS - 1 :], edge)
        upper = jnp.where(row == CRS - 1, edge, pltpu.roll(here, CRS - 1, 0))
        power = (0.5 * (upper - lower)) ** 2
        earlier = jnp.where(col == 0, here, pltpu.roll(here, 1, 1))
        later = jnp.where(col == NT - 1, here, pltpu.roll(here, NT - 1, 1))
        power = power + (0.5 * (later - earlier)) ** 2
        if 0 < i < INL - 1:
            power = conductivity(power + (0.5 * (vol[i + 1] - vol[i - 1])) ** 2)
        partial[i] = power
        for t in range(TILES):
            cells_v[pl.ds(i * TILES + t, CRS, stride=ROWS), :] = here[:, lane_tile(t)]


def prepare_kernel(
    axes, vol, partial, cells_v, wide1, wide0, cond, wide_out, narrow_out, cells_c
):
    rank = lax.axis_index(axes[0])
    even = lax.rem(rank, 2) == 0
    for i in range(INL):
        value = partial[i]
        if i == 0:
            up = jnp.where(even, wide1[0], wide0[0])
            up = jnp.where(rank == 0, vol[0], up)
            value = conductivity(value + (0.5 * (vol[1] - up)) ** 2)
        if i == INL - 1:
            down = jnp.where(even, wide0[0], wide1[0])
            down = jnp.where(rank == WIDE - 1, vol[INL - 1], down)
            value = conductivity(value + (0.5 * (down - vol[INL - 2])) ** 2)
        cond[i] = value
        for t in range(TILES):
            where = pl.ds(i * TILES + t, CRS, stride=ROWS)
            cells_c[where, :] = value[:, lane_tile(t)]
    ones = jnp.ones((ROWS, LANES), jnp.float32)
    v = [cells_v[pl.ds(c * ROWS, ROWS), :] for c in range(CRS)]
    k = [cells_c[pl.ds(c * ROWS, ROWS), :] for c in range(CRS)]
    m0, d0, m1, d1, g, _ = condense([ones] * CRS, v, links(k))
    for p, value in enumerate((g, m0, m1, d0, d1, k[0], k[-1])):
        narrow_out[p * ROWS : (p + 1) * ROWS, :] = value
    ones = jnp.ones((GROUP, LANES), jnp.float32)
    for t in range(TILES):
        for u in range(CRS // GROUP):
            at = (slice(u * GROUP, (u + 1) * GROUP), lane_tile(t))
            v = [vol[(i, *at)] for i in range(INL)]
            k = [cond[(i, *at)] for i in range(INL)]
            _, d0, _, d1, _, _ = condense([ones] * INL, v, links(k))
            for p, value in enumerate((*k, d0, d1)):
                start = t * GROUP * 2 * WPORTS + p * 2 + u
                wide_out[pl.ds(start, GROUP, stride=2 * WPORTS), :] = value


def sublane_shift(x, s):
    return pltpu.roll(x, s % GROUP, 0)


def wide_kernel(ports, out):
    part = WIDE // GROUP
    sub = iota((GROUP, LANES), 0)
    zero = jnp.zeros((GROUP, LANES), jnp.float32)
    ones = jnp.ones((GROUP, LANES), jnp.float32)
    for u in range(2):

        def port(p, j):
            return ports[pl.ds(j * 2 * WPORTS + p * 2 + u, GROUP, stride=part * 2 * WPORTS), :]

        last_cond = sublane_shift(port(INL - 1, part - 1), 1)
        mass, rhs, link = [zero], [zero], []
        for j in range(part):
            k = [port(p, j) for p in range(INL)]
            joined = half_weight * (last_cond + k[0])
            if j == 0:
                joined = jnp.where(sub == 0, 0.0, joined)
            m0, _, m1, _, g, _ = condense([ones] * INL, [zero] * INL, links(k))
            link += [joined, g]
            mass += [m0, m1]
            rhs += [port(INL, j), port(INL + 1, j)]
            last_cond = k[-1]
        count = len(mass)
        m0, d0, m1, d1, g, steps = condense(mass, rhs, link)
        last = halving(
            m1 + sublane_shift(m0, -1),
            d1 + sublane_shift(d0, -1),
            g,
            sublane_shift(g, -1),
            sublane_shift,
            GROUP,
        )
        x = expand(sublane_shift(last, 1), last, steps, count)
        for j in range(part):
            for e in range(2):
                out[pl.ds(j * 4 + e * 2 + u, GROUP, stride=part * 4), :] = x[1 + 2 * j + e]


def time_kernel(vol, cond, out, cells_v, cells_c, link_s, tmp):
    lines = INL * CRS
    half = NT // 2
    blocks = half // LANES
    for b in range(blocks):
        for source, cells in ((vol, cells_v), (cond, cells_c)):
            stacked = jnp.concatenate(
                [
                    source[:, :, b * LANES : (b + 1) * LANES].reshape(lines, LANES),
                    source[:, :, half + b * LANES : half + (b + 1) * LANES].reshape(lines, LANES),
                ],
                0,
            )
            cells[b * LANES : (b + 1) * LANES, :] = stacked.T
    lane = iota((GROUP, LANES), 1)
    sub = iota((GROUP, LANES), 0)
    low = lane < lines

    def swap(x):
        return pltpu.roll(x, lines, 1)

    for s in range(half // GROUP):
        here = cells_c[s * GROUP : (s + 1) * GROUP, :]
        if s:
            edge = cells_c[s * GROUP - 1 : s * GROUP, :]
        else:
            edge = swap(cells_c[half - GROUP : half, :])[GROUP - 1 :]
        value = half_weight * (here + jnp.where(sub == 0, edge, pltpu.roll(here, 1, 0)))
        if s == 0:
            value = jnp.where((sub == 0) & low, 0.0, value)
        link_s[s * GROUP : (s + 1) * GROUP, :] = value

    def chain_shift(x, s):
        n = x.shape[0]
        if abs(s) == n:
            return swap(x)
        rolled = pltpu.roll(x, s % n, 0)
        place = iota(x.shape, 0)
        wrapped = place < s if s > 0 else place >= n + s
        return jnp.where(wrapped, swap(rolled), rolled)

    runs = half // GROUP
    zero = jnp.zeros((runs, LANES), jnp.float32)
    ones = jnp.ones((runs, LANES), jnp.float32)
    v = [cells_v[pl.ds(k, runs, stride=GROUP), :] for k in range(GROUP)]
    link = [link_s[pl.ds(k, runs, stride=GROUP), :] for k in range(GROUP)]
    m0, d0, m1, d1, g, steps = condense([zero] + [ones] * GROUP, [zero] + v, link)
    tmp[0] = m1 + chain_shift(m0, -1)
    tmp[1] = d1 + chain_shift(d0, -1)
    tmp[2] = g
    zero = jnp.zeros((GROUP, LANES), jnp.float32)

    def take(p):
        return [tmp[p, pl.ds(k, GROUP, stride=GROUP), :] for k in range(GROUP)]

    m0, d0, m1, d1, g, inner = condense([zero] + take(0), [zero] + take(1), take(2))
    last = halving(
        m1 + chain_shift(m0, -1),
        d1 + chain_shift(d0, -1),
        g,
        chain_shift(g, -1),
        chain_shift,
        2 * GROUP,
    )
    x = expand(chain_shift(last, 1), last, inner, GROUP + 1)
    for k in range(GROUP):
        tmp[0, pl.ds(k, GROUP, stride=GROUP), :] = x[k + 1]
    last = tmp[0]
    x = expand(chain_shift(last, 1), last, steps, GROUP + 1)
    for k in range(GROUP):
        cells_v[pl.ds(k, runs, stride=GROUP), :] = x[k + 1]
    for b in range(blocks):
        turned = cells_v[b * LANES : (b + 1) * LANES, :].T
        for h in range(2):
            out[:, :, h * half + b * LANES : h * half + (b + 1) * LANES] = turned[
                h * lines : (h + 1) * lines
            ].reshape(INL, CRS, LANES)


def ports_of(ref):
    return [ref[p * ROWS : (p + 1) * ROWS, :] for p in range(PORTS)]


def chain_of(ports):
    mass, rhs, link = [], [], []
    for n, (g, m0, m1, d0, d1, _, _) in enumerate(ports):
        mass += [m0, m1]
        rhs += [d0, d1]
        link.append(g)
        if n < len(ports) - 1:
            link.append(half_weight * (ports[n][6] + ports[n + 1][5]))
    return mass, rhs, link


def in_order(mine, theirs, first):
    return [
        [jnp.where(first, a, b) for a, b in zip(mine, theirs)],
        [jnp.where(first, b, a) for a, b in zip(mine, theirs)],
    ]


def places(axes):
    rank = lax.axis_index(axes[1])
    return lax.rem(rank, 2) == 0, lax.rem(rank, RUN) < 2, rank < RUN


def join_kernel(axes, own, beside, joined):
    pair = in_order(ports_of(own), ports_of(beside), places(axes)[0])
    m0, d0, m1, d1, g, _ = condense(*chain_of(pair))
    for p, value in enumerate((g, m0, m1, d0, d1, pair[0][5], pair[1][6])):
        joined[p * ROWS : (p + 1) * ROWS, :] = value


def facing(run, low):
    m0, d0, m1, d1, g, steps = condense(*chain_of(run))
    here_m, here_d = jnp.where(low, m1, m0), jnp.where(low, d1, d0)
    away_m, away_d = jnp.where(low, m0, m1), jnp.where(low, d0, d1)
    inverse = 1.0 / (g + away_m)
    slope, base = g * inverse, away_d * inverse
    edge = (here_m + slope * away_m, here_d + slope * away_d, jnp.where(low, run[-1][6], run[0][5]))
    return (slope, base, steps), edge


def edge_kernel(axes, joined, across, out):
    _, second, low = places(axes)
    _, edge = facing(in_order(ports_of(joined), ports_of(across), second), low)
    for p, value in enumerate(edge):
        out[p * ROWS : (p + 1) * ROWS, :] = value


def half_of(x, first):
    return jnp.where(first, x[0], x[2]), jnp.where(first, x[1], x[3])


def cross_kernel(
    axes, own, beside, joined, across, other, cells_v, cells_c, timed, out, cells_x
):
    first, second, low = places(axes)
    run = in_order(ports_of(joined), ports_of(across), second)
    (slope, base, steps), (m0, d0, c0) = facing(run, low)
    m1, d1, c1 = [other[p * ROWS : (p + 1) * ROWS, :] for p in range(3)]
    link = half_weight * (c0 + c1)
    here = (d0 * (m1 + link) + link * d1) / (m0 * m1 + link * (m0 + m1))
    away = base + slope * here
    x = expand(jnp.where(low, away, here), jnp.where(low, here, away), steps, 4)
    steps = condense(*chain_of(in_order(ports_of(own), ports_of(beside), first)))[-1]
    x = expand(*half_of(x, second), steps, 4)
    v = [cells_v[pl.ds(c * ROWS, ROWS), :] for c in range(CRS)]
    k = [cells_c[pl.ds(c * ROWS, ROWS), :] for c in range(CRS)]
    ones = jnp.ones((ROWS, LANES), jnp.float32)
    steps = condense([ones] * CRS, v, links(k))[-1]
    x = expand(*half_of(x, first), steps, CRS)
    for c in range(CRS):
        cells_x[c * ROWS : (c + 1) * ROWS, :] = x[c]
    for i in range(INL):
        for t in range(TILES):
            out[i, :, lane_tile(t)] = (
                timed[i, :, lane_tile(t)] + cells_x[pl.ds(i * TILES + t, CRS, stride=ROWS), :]
            )


def finish_kernel(vol, cond, ends, others, out):
    ones = jnp.ones((GROUP, LANES), jnp.float32)
    for t in range(TILES):
        for u in range(CRS // GROUP):
            at = (slice(u * GROUP, (u + 1) * GROUP), lane_tile(t))
            v = [vol[(i, *at)] for i in range(INL)]
            k = [cond[(i, *at)] for i in range(INL)]
            steps = condense([ones] * INL, v, links(k))[-1]
            first = ends[pl.ds(t * GROUP * 4 + u, GROUP, stride=4), :]
            last = ends[pl.ds(t * GROUP * 4 + 2 + u, GROUP, stride=4), :]
            for i, x in enumerate(expand(first, last, steps, INL)):
                out[(i, *at)] = (x + others[(i, *at)]) * (1.0 / 3.0)


def f32(*shape):
    return jax.ShapeDtypeStruct(shape, jnp.float32)


def call(kernel, out, *args, scratch=()):
    return pl.pallas_call(
        kernel,
        out_shape=out,
        scratch_shapes=[pltpu.VMEM(s, jnp.float32) for s in scratch],
        compiler_params=pltpu.CompilerParams(vmem_limit_bytes=16 * 2**20),
    )(*args)


def per_device(axes, volume):
    wide_axes, narrow_axes = axes

    def exchanged(layer, axis, count, start):
        pairs = [(i, i + 1) for i in range(start, count - 1, 2)]
        return lax.ppermute(layer, axis, pairs + [(j, i) for i, j in pairs])

    inline_face, longer = f32(1, CRS, NT), f32(CRS + 1, 1, NT)
    narrow1, wide1, narrow0, wide0 = call(
        lambda *refs: faces_kernel(axes, *refs),
        (longer, inline_face, longer, inline_face),
        volume,
    )
    narrow1 = exchanged(narrow1, narrow_axes, NARROW, 1)
    wide1 = exchanged(wide1, wide_axes, WIDE, 1)
    narrow0 = exchanged(narrow0, narrow_axes, NARROW, 0)
    wide0 = exchanged(wide0, wide_axes, WIDE, 0)
    cells = CRS * ROWS
    partial, cells_v = call(
        lambda *refs: partial_kernel(axes, *refs),
        (f32(INL, CRS, NT), f32(cells, LANES)),
        volume,
        narrow1,
        narrow0,
    )
    cond, wide_ports, narrow_ports, cells_c = call(
        lambda *refs: prepare_kernel(axes, *refs),
        (
            f32(INL, CRS, NT),
            f32(WIDE * WPORTS * 2, LANES),
            f32(PORTS * ROWS, LANES),
            f32(cells, LANES),
        ),
        volume,
        partial,
        cells_v,
        wide1,
        wide0,
    )
    lines = lax.all_to_all(
        wide_ports.reshape(WIDE, WPORTS, 2, LANES), wide_axes, split_axis=0, concat_axis=0, tiled=True
    )

    def swapped(x, step):
        return lax.ppermute(x, narrow_axes, [(n, n ^ step) for n in range(NARROW)])

    beside = swapped(narrow_ports, 1)
    joined = call(
        lambda *refs: join_kernel(axes, *refs), f32(PORTS * ROWS, LANES), narrow_ports, beside
    )
    across = swapped(joined, 3)
    edge = call(lambda *refs: edge_kernel(axes, *refs), f32(3 * ROWS, LANES), joined, across)
    other = swapped(edge, RUN)
    timed = call(
        time_kernel,
        f32(INL, CRS, NT),
        volume,
        cond,
        scratch=(
            (NT // 2, LANES),
            (NT // 2, LANES),
            (NT // 2, LANES),
            (3, NT // 2 // GROUP, LANES),
        ),
    )
    lines, edge = lax.optimization_barrier((lines, edge))
    solved = call(
        wide_kernel, f32(WIDE * 4, LANES), lines.reshape(WIDE * WPORTS * 2, LANES)
    )
    ends = lax.all_to_all(
        solved.reshape(WIDE, 2, 2, LANES), wide_axes, split_axis=0, concat_axis=0, tiled=True
    )
    others = call(
        lambda *refs: cross_kernel(axes, *refs),
        f32(INL, CRS, NT),
        narrow_ports,
        beside,
        joined,
        across,
        other,
        cells_v,
        cells_c,
        timed,
        scratch=((cells, LANES),),
    )
    return call(
        finish_kernel, f32(INL, CRS, NT), volume, cond, ends.reshape(WIDE * 4, LANES), others
    )


def solution(mesh):
    axes = ("wide", "narrow")
    return jax.shard_map(
        lambda volume: per_device(axes, volume),
        mesh=mesh,
        in_specs=(P("wide", "narrow", None),),
        out_specs=P("wide", "narrow", None),
        check_vma=False,
    )
```

```python
import jax
import jax.numpy as jnp
from jax import lax
from jax.experimental import pallas as pl
from jax.experimental.pallas import tpu as pltpu
from jax.sharding import PartitionSpec as P

half_weight = 150.0
contrast_sq = 9.0

WIDE = 64
NARROW = 8
INL = 4
CRS = 16
NT = 1024
LANES = 128
TILES = NT // LANES
ROWS = INL * TILES
GROUP = 8
PORTS = 7
WPORTS = INL + 2
RUN = 4


def condense(mass, rhs, link):
    mass, rhs, right = list(mass), list(rhs), list(link)
    alive, steps = list(range(len(mass))), []
    while len(alive) > 2:
        gone = set()
        for at in range(1, len(alive) - 1, 2):
            l, k, r = alive[at - 1 : at + 2]
            inverse = 1.0 / (right[l] + right[k] + mass[k])
            to_left, to_right = right[l] * inverse, right[k] * inverse
            mass[l] = mass[l] + to_left * mass[k]
            rhs[l] = rhs[l] + to_left * rhs[k]
            mass[r] = mass[r] + to_right * mass[k]
            rhs[r] = rhs[r] + to_right * rhs[k]
            right[l] = to_left * right[k]
            steps.append((l, k, r, to_left, to_right, rhs[k] * inverse))
            gone.add(k)
        alive = [k for k in alive if k not in gone]
    return mass[0], rhs[0], mass[-1], rhs[-1], right[0], steps


def expand(first, last, steps, count):
    x = [None] * count
    x[0], x[-1] = first, last
    for l, k, r, to_left, to_right, base in reversed(steps):
        x[k] = base + to_left * x[l] + to_right * x[r]
    return x


def links(cond):
    return [half_weight * (a + b) for a, b in zip(cond[:-1], cond[1:])]


def halving(mass, rhs, before, after, shift, count):
    step = 1
    while step < count:
        inverse = 1.0 / (before + after + mass)
        to_left, to_right = before * inverse, after * inverse
        across = to_left * after
        mass, rhs = (
            mass + shift(to_right * mass, step) + shift(to_left * mass, -step),
            rhs + shift(to_right * rhs, step) + shift(to_left * rhs, -step),
        )
        before, after = shift(across, step), shift(across, -step)
        step *= 2
    return rhs / mass


def iota(shape, dim):
    return lax.broadcasted_iota(jnp.int32, shape, dim)


def lane_tile(t):
    return slice(t * LANES, (t + 1) * LANES)


def faces_kernel(axes, vol, narrow1, wide1, narrow0, wide0):
    wide_even, narrow_even = [lax.rem(lax.axis_index(axis), 2) == 0 for axis in axes]
    first, last = vol[0], vol[INL - 1]
    wide1[0] = jnp.where(wide_even, first, last)
    wide0[0] = jnp.where(wide_even, last, first)
    for i in range(INL):
        first, last = vol[i, :1], vol[i, CRS - 1 :]
        narrow1[i] = jnp.where(narrow_even, first, last)
        narrow0[i] = jnp.where(narrow_even, last, first)
    for ref in (narrow1, narrow0):
        ref[INL:] = jnp.zeros((CRS + 1 - INL, 1, NT), jnp.float32)


def conductivity(power):
    return contrast_sq / (contrast_sq + power)


def partial_kernel(axes, vol, narrow1, narrow0, partial, cells_v):
    rank = lax.axis_index(axes[1])
    even = lax.rem(rank, 2) == 0
    col = iota((CRS, NT), 1)
    row = iota((CRS, NT), 0)
    for i in range(INL):
        here = vol[i]
        edge = jnp.where(even, narrow1[i], narrow0[i])
        edge = jnp.where(rank == 0, here[:1], edge)
        lower = jnp.where(row == 0, edge, pltpu.roll(here, 1, 0))
        edge = jnp.where(even, narrow0[i], narrow1[i])
        edge = jnp.where(rank == NARROW - 1, here[CRS - 1 :], edge)
        upper = jnp.where(row == CRS - 1, edge, pltpu.roll(here, CRS - 1, 0))
        power = (0.5 * (upper - lower)) ** 2
        earlier = jnp.where(col == 0, here, pltpu.roll(here, 1, 1))
        later = jnp.where(col == NT - 1, here, pltpu.roll(here, NT - 1, 1))
        power = power + (0.5 * (later - earlier)) ** 2
        if 0 < i < INL - 1:
            power = conductivity(power + (0.5 * (vol[i + 1] - vol[i - 1])) ** 2)
        partial[i] = power
        for t in range(TILES):
            cells_v[pl.ds(i * TILES + t, CRS, stride=ROWS), :] = here[:, lane_tile(t)]


def prepare_kernel(
    axes, vol, partial, cells_v, wide1, wide0, cond, wide_out, narrow_out, cells_c
):
    rank = lax.axis_index(axes[0])
    even = lax.rem(rank, 2) == 0
    for i in range(INL):
        value = partial[i]
        if i == 0:
            up = jnp.where(even, wide1[0], wide0[0])
            up = jnp.where(rank == 0, vol[0], up)
            value = conductivity(value + (0.5 * (vol[1] - up)) ** 2)
        if i == INL - 1:
            down = jnp.where(even, wide0[0], wide1[0])
            down = jnp.where(rank == WIDE - 1, vol[INL - 1], down)
            value = conductivity(value + (0.5 * (down - vol[INL - 2])) ** 2)
        cond[i] = value
        for t in range(TILES):
            where = pl.ds(i * TILES + t, CRS, stride=ROWS)
            cells_c[where, :] = value[:, lane_tile(t)]
    ones = jnp.ones((ROWS, LANES), jnp.float32)
    v = [cells_v[pl.ds(c * ROWS, ROWS), :] for c in range(CRS)]
    k = [cells_c[pl.ds(c * ROWS, ROWS), :] for c in range(CRS)]
    m0, d0, m1, d1, g, _ = condense([ones] * CRS, v, links(k))
    for p, value in enumerate((g, m0, m1, d0, d1, k[0], k[-1])):
        narrow_out[p * ROWS : (p + 1) * ROWS, :] = value
    ones = jnp.ones((GROUP, LANES), jnp.float32)
    for t in range(TILES):
        for u in range(CRS // GROUP):
            at = (slice(u * GROUP, (u + 1) * GROUP), lane_tile(t))
            v = [vol[(i, *at)] for i in range(INL)]
            k = [cond[(i, *at)] for i in range(INL)]
            _, d0, _, d1, _, _ = condense([ones] * INL, v, links(k))
            for p, value in enumerate((*k, d0, d1)):
                start = t * GROUP * 2 * WPORTS + p * 2 + u
                wide_out[pl.ds(start, GROUP, stride=2 * WPORTS), :] = value


def sublane_shift(x, s):
    return pltpu.roll(x, s % GROUP, 0)


def wide_kernel(ports, out):
    part = WIDE // GROUP
    sub = iota((GROUP, LANES), 0)
    zero = jnp.zeros((GROUP, LANES), jnp.float32)
    ones = jnp.ones((GROUP, LANES), jnp.float32)
    for u in range(2):

        def port(p, j):
            return ports[pl.ds(j * 2 * WPORTS + p * 2 + u, GROUP, stride=part * 2 * WPORTS), :]

        last_cond = sublane_shift(port(INL - 1, part - 1), 1)
        mass, rhs, link = [zero], [zero], []
        for j in range(part):
            k = [port(p, j) for p in range(INL)]
            joined = half_weight * (last_cond + k[0])
            if j == 0:
                joined = jnp.where(sub == 0, 0.0, joined)
            m0, _, m1, _, g, _ = condense([ones] * INL, [zero] * INL, links(k))
            link += [joined, g]
            mass += [m0, m1]
            rhs += [port(INL, j), port(INL + 1, j)]
            last_cond = k[-1]
        count = len(mass)
        m0, d0, m1, d1, g, steps = condense(mass, rhs, link)
        last = halving(
            m1 + sublane_shift(m0, -1),
            d1 + sublane_shift(d0, -1),
            g,
            sublane_shift(g, -1),
            sublane_shift,
            GROUP,
        )
        x = expand(sublane_shift(last, 1), last, steps, count)
        for j in range(part):
            for e in range(2):
                out[pl.ds(j * 4 + e * 2 + u, GROUP, stride=part * 4), :] = x[1 + 2 * j + e]


def time_kernel(vol, cond, out, inner, cells_v, cells_c, link_s, tmp):
    ones = jnp.ones((GROUP, LANES), jnp.float32)
    for t in range(TILES):
        for u in range(CRS // GROUP):
            at = (slice(u * GROUP, (u + 1) * GROUP), lane_tile(t))
            v = [vol[(i, *at)] for i in range(INL)]
            k = [cond[(i, *at)] for i in range(INL)]
            near, far = condense([ones] * INL, v, links(k))[-1]
            _, _, _, a1, c1, b1 = near
            _, _, _, a2, c2, b2 = far
            found = (b1 + c1 * b2, a1 + c1 * a2, c1 * c2, b2, a2, c2)
            for p, value in enumerate(found):
                inner[(p, *at)] = value
    lines = INL * CRS
    half = NT // 2
    blocks = half // LANES
    for b in range(blocks):
        for source, cells in ((vol, cells_v), (cond, cells_c)):
            stacked = jnp.concatenate(
                [
                    source[:, :, b * LANES : (b + 1) * LANES].reshape(lines, LANES),
                    source[:, :, half + b * LANES : half + (b + 1) * LANES].reshape(lines, LANES),
                ],
                0,
            )
            cells[b * LANES : (b + 1) * LANES, :] = stacked.T
    lane = iota((GROUP, LANES), 1)
    sub = iota((GROUP, LANES), 0)
    low = lane < lines

    def swap(x):
        return pltpu.roll(x, lines, 1)

    for s in range(half // GROUP):
        here = cells_c[s * GROUP : (s + 1) * GROUP, :]
        if s:
            edge = cells_c[s * GROUP - 1 : s * GROUP, :]
        else:
            edge = swap(cells_c[half - GROUP : half, :])[GROUP - 1 :]
        value = half_weight * (here + jnp.where(sub == 0, edge, pltpu.roll(here, 1, 0)))
        if s == 0:
            value = jnp.where((sub == 0) & low, 0.0, value)
        link_s[s * GROUP : (s + 1) * GROUP, :] = value

    def chain_shift(x, s):
        n = x.shape[0]
        if abs(s) == n:
            return swap(x)
        rolled = pltpu.roll(x, s % n, 0)
        place = iota(x.shape, 0)
        wrapped = place < s if s > 0 else place >= n + s
        return jnp.where(wrapped, swap(rolled), rolled)

    runs = half // GROUP
    zero = jnp.zeros((runs, LANES), jnp.float32)
    ones = jnp.ones((runs, LANES), jnp.float32)
    v = [cells_v[pl.ds(k, runs, stride=GROUP), :] for k in range(GROUP)]
    link = [link_s[pl.ds(k, runs, stride=GROUP), :] for k in range(GROUP)]
    m0, d0, m1, d1, g, steps = condense([zero] + [ones] * GROUP, [zero] + v, link)
    tmp[0] = m1 + chain_shift(m0, -1)
    tmp[1] = d1 + chain_shift(d0, -1)
    tmp[2] = g
    zero = jnp.zeros((GROUP, LANES), jnp.float32)

    def take(p):
        return [tmp[p, pl.ds(k, GROUP, stride=GROUP), :] for k in range(GROUP)]

    m0, d0, m1, d1, g, inner = condense([zero] + take(0), [zero] + take(1), take(2))
    last = halving(
        m1 + chain_shift(m0, -1),
        d1 + chain_shift(d0, -1),
        g,
        chain_shift(g, -1),
        chain_shift,
        2 * GROUP,
    )
    x = expand(chain_shift(last, 1), last, inner, GROUP + 1)
    for k in range(GROUP):
        tmp[0, pl.ds(k, GROUP, stride=GROUP), :] = x[k + 1]
    last = tmp[0]
    x = expand(chain_shift(last, 1), last, steps, GROUP + 1)
    for k in range(GROUP):
        cells_v[pl.ds(k, runs, stride=GROUP), :] = x[k + 1]
    for b in range(blocks):
        turned = cells_v[b * LANES : (b + 1) * LANES, :].T
        for h in range(2):
            out[:, :, h * half + b * LANES : h * half + (b + 1) * LANES] = turned[
                h * lines : (h + 1) * lines
            ].reshape(INL, CRS, LANES)


def ports_of(ref):
    return [ref[p * ROWS : (p + 1) * ROWS, :] for p in range(PORTS)]


def chain_of(ports):
    mass, rhs, link = [], [], []
    for n, (g, m0, m1, d0, d1, _, _) in enumerate(ports):
        mass += [m0, m1]
        rhs += [d0, d1]
        link.append(g)
        if n < len(ports) - 1:
            link.append(half_weight * (ports[n][6] + ports[n + 1][5]))
    return mass, rhs, link


def in_order(mine, theirs, first):
    return [
        [jnp.where(first, a, b) for a, b in zip(mine, theirs)],
        [jnp.where(first, b, a) for a, b in zip(mine, theirs)],
    ]


def places(axes):
    rank = lax.axis_index(axes[1])
    return lax.rem(rank, 2) == 0, lax.rem(rank, RUN) < 2, rank < RUN


def join_kernel(axes, own, beside, joined):
    pair = in_order(ports_of(own), ports_of(beside), places(axes)[0])
    m0, d0, m1, d1, g, _ = condense(*chain_of(pair))
    for p, value in enumerate((g, m0, m1, d0, d1, pair[0][5], pair[1][6])):
        joined[p * ROWS : (p + 1) * ROWS, :] = value


def facing(run, low):
    m0, d0, m1, d1, g, steps = condense(*chain_of(run))
    here_m, here_d = jnp.where(low, m1, m0), jnp.where(low, d1, d0)
    away_m, away_d = jnp.where(low, m0, m1), jnp.where(low, d0, d1)
    inverse = 1.0 / (g + away_m)
    slope, base = g * inverse, away_d * inverse
    edge = (here_m + slope * away_m, here_d + slope * away_d, jnp.where(low, run[-1][6], run[0][5]))
    return (slope, base, steps), edge


def edge_kernel(axes, joined, across, out):
    _, second, low = places(axes)
    _, edge = facing(in_order(ports_of(joined), ports_of(across), second), low)
    for p, value in enumerate(edge):
        out[p * ROWS : (p + 1) * ROWS, :] = value


def half_of(x, first):
    return jnp.where(first, x[0], x[2]), jnp.where(first, x[1], x[3])


def cross_kernel(
    axes, own, beside, joined, across, other, cells_v, cells_c, timed, out, cells_x
):
    first, second, low = places(axes)
    run = in_order(ports_of(joined), ports_of(across), second)
    (slope, base, steps), (m0, d0, c0) = facing(run, low)
    m1, d1, c1 = [other[p * ROWS : (p + 1) * ROWS, :] for p in range(3)]
    link = half_weight * (c0 + c1)
    here = (d0 * (m1 + link) + link * d1) / (m0 * m1 + link * (m0 + m1))
    away = base + slope * here
    x = expand(jnp.where(low, away, here), jnp.where(low, here, away), steps, 4)
    steps = condense(*chain_of(in_order(ports_of(own), ports_of(beside), first)))[-1]
    x = expand(*half_of(x, second), steps, 4)
    v = [cells_v[pl.ds(c * ROWS, ROWS), :] for c in range(CRS)]
    k = [cells_c[pl.ds(c * ROWS, ROWS), :] for c in range(CRS)]
    ones = jnp.ones((ROWS, LANES), jnp.float32)
    steps = condense([ones] * CRS, v, links(k))[-1]
    x = expand(*half_of(x, first), steps, CRS)
    for c in range(CRS):
        cells_x[c * ROWS : (c + 1) * ROWS, :] = x[c]
    for i in range(INL):
        for t in range(TILES):
            out[i, :, lane_tile(t)] = (
                timed[i, :, lane_tile(t)] + cells_x[pl.ds(i * TILES + t, CRS, stride=ROWS), :]
            )


def finish_kernel(inner, ends, others, out):
    for t in range(TILES):
        for u in range(CRS // GROUP):
            at = (slice(u * GROUP, (u + 1) * GROUP), lane_tile(t))
            first = ends[pl.ds(t * GROUP * 4 + u, GROUP, stride=4), :]
            last = ends[pl.ds(t * GROUP * 4 + 2 + u, GROUP, stride=4), :]
            base, to_first, to_last, base2, to_first2, to_last2 = [
                inner[(p, *at)] for p in range(6)
            ]
            second = base + to_first * first + to_last * last
            third = base2 + to_first2 * first + to_last2 * last
            for i, x in enumerate((first, second, third, last)):
                out[(i, *at)] = (x + others[(i, *at)]) * (1.0 / 3.0)


def f32(*shape):
    return jax.ShapeDtypeStruct(shape, jnp.float32)


def call(kernel, out, *args, scratch=()):
    return pl.pallas_call(
        kernel,
        out_shape=out,
        scratch_shapes=[pltpu.VMEM(s, jnp.float32) for s in scratch],
        compiler_params=pltpu.CompilerParams(vmem_limit_bytes=16 * 2**20),
    )(*args)


def per_device(axes, volume):
    wide_axes, narrow_axes = axes

    def exchanged(layer, axis, count, start):
        pairs = [(i, i + 1) for i in range(start, count - 1, 2)]
        return lax.ppermute(layer, axis, pairs + [(j, i) for i, j in pairs])

    inline_face, longer = f32(1, CRS, NT), f32(CRS + 1, 1, NT)
    narrow1, wide1, narrow0, wide0 = call(
        lambda *refs: faces_kernel(axes, *refs),
        (longer, inline_face, longer, inline_face),
        volume,
    )
    narrow1 = exchanged(narrow1, narrow_axes, NARROW, 1)
    wide1 = exchanged(wide1, wide_axes, WIDE, 1)
    narrow0 = exchanged(narrow0, narrow_axes, NARROW, 0)
    wide0 = exchanged(wide0, wide_axes, WIDE, 0)
    cells = CRS * ROWS
    partial, cells_v = call(
        lambda *refs: partial_kernel(axes, *refs),
        (f32(INL, CRS, NT), f32(cells, LANES)),
        volume,
        narrow1,
        narrow0,
    )
    cond, wide_ports, narrow_ports, cells_c = call(
        lambda *refs: prepare_kernel(axes, *refs),
        (
            f32(INL, CRS, NT),
            f32(WIDE * WPORTS * 2, LANES),
            f32(PORTS * ROWS, LANES),
            f32(cells, LANES),
        ),
        volume,
        partial,
        cells_v,
        wide1,
        wide0,
    )
    lines = lax.all_to_all(
        wide_ports.reshape(WIDE, WPORTS, 2, LANES), wide_axes, split_axis=0, concat_axis=0, tiled=True
    )

    def swapped(x, step):
        return lax.ppermute(x, narrow_axes, [(n, n ^ step) for n in range(NARROW)])

    beside = swapped(narrow_ports, 1)
    joined = call(
        lambda *refs: join_kernel(axes, *refs), f32(PORTS * ROWS, LANES), narrow_ports, beside
    )
    across = swapped(joined, 3)
    edge = call(lambda *refs: edge_kernel(axes, *refs), f32(3 * ROWS, LANES), joined, across)
    other = swapped(edge, RUN)
    timed, inner = call(
        time_kernel,
        (f32(INL, CRS, NT), f32(6, CRS, NT)),
        volume,
        cond,
        scratch=(
            (NT // 2, LANES),
            (NT // 2, LANES),
            (NT // 2, LANES),
            (3, NT // 2 // GROUP, LANES),
        ),
    )
    lines, edge = lax.optimization_barrier((lines, edge))
    solved = call(
        wide_kernel, f32(WIDE * 4, LANES), lines.reshape(WIDE * WPORTS * 2, LANES)
    )
    ends = lax.all_to_all(
        solved.reshape(WIDE, 2, 2, LANES), wide_axes, split_axis=0, concat_axis=0, tiled=True
    )
    others = call(
        lambda *refs: cross_kernel(axes, *refs),
        f32(INL, CRS, NT),
        narrow_ports,
        beside,
        joined,
        across,
        other,
        cells_v,
        cells_c,
        timed,
        scratch=((cells, LANES),),
    )
    return call(
        finish_kernel, f32(INL, CRS, NT), inner, ends.reshape(WIDE * 4, LANES), others
    )


def solution(mesh):
    axes = ("wide", "narrow")
    return jax.shard_map(
        lambda volume: per_device(axes, volume),
        mesh=mesh,
        in_specs=(P("wide", "narrow", None),),
        out_specs=P("wide", "narrow", None),
        check_vma=False,
    )
```

```python
import jax
import jax.numpy as jnp
from jax import lax
from jax.experimental import pallas as pl
from jax.experimental.pallas import tpu as pltpu
from jax.sharding import PartitionSpec as P

half_weight = 150.0
contrast_sq = 9.0

WIDE = 64
NARROW = 8
INL = 4
CRS = 16
NT = 1024
LANES = 128
TILES = NT // LANES
ROWS = INL * TILES
GROUP = 8
PORTS = 7
WPORTS = INL + 2
RUN = 4


def condense(mass, rhs, link):
    mass, rhs, right = list(mass), list(rhs), list(link)
    alive, steps = list(range(len(mass))), []
    while len(alive) > 2:
        gone = set()
        for at in range(1, len(alive) - 1, 2):
            l, k, r = alive[at - 1 : at + 2]
            inverse = 1.0 / (right[l] + right[k] + mass[k])
            to_left, to_right = right[l] * inverse, right[k] * inverse
            mass[l] = mass[l] + to_left * mass[k]
            rhs[l] = rhs[l] + to_left * rhs[k]
            mass[r] = mass[r] + to_right * mass[k]
            rhs[r] = rhs[r] + to_right * rhs[k]
            right[l] = to_left * right[k]
            steps.append((l, k, r, to_left, to_right, rhs[k] * inverse))
            gone.add(k)
        alive = [k for k in alive if k not in gone]
    return mass[0], rhs[0], mass[-1], rhs[-1], right[0], steps


def expand(first, last, steps, count):
    x = [None] * count
    x[0], x[-1] = first, last
    for l, k, r, to_left, to_right, base in reversed(steps):
        x[k] = base + to_left * x[l] + to_right * x[r]
    return x


def links(cond):
    return [half_weight * (a + b) for a, b in zip(cond[:-1], cond[1:])]


def halving(mass, rhs, before, after, shift, count):
    step = 1
    while step < count:
        inverse = 1.0 / (before + after + mass)
        to_left, to_right = before * inverse, after * inverse
        across = to_left * after
        mass, rhs = (
            mass + shift(to_right * mass, step) + shift(to_left * mass, -step),
            rhs + shift(to_right * rhs, step) + shift(to_left * rhs, -step),
        )
        before, after = shift(across, step), shift(across, -step)
        step *= 2
    return rhs / mass


def iota(shape, dim):
    return lax.broadcasted_iota(jnp.int32, shape, dim)


def lane_tile(t):
    return slice(t * LANES, (t + 1) * LANES)


def faces_kernel(axes, vol, narrow1, wide1, narrow0, wide0):
    wide_even, narrow_even = [lax.rem(lax.axis_index(axis), 2) == 0 for axis in axes]
    first, last = vol[0], vol[INL - 1]
    wide1[0] = jnp.where(wide_even, first, last)
    wide0[0] = jnp.where(wide_even, last, first)
    for i in range(INL):
        first, last = vol[i, :1], vol[i, CRS - 1 :]
        narrow1[i] = jnp.where(narrow_even, first, last)
        narrow0[i] = jnp.where(narrow_even, last, first)
    for ref in (narrow1, narrow0):
        ref[INL:] = jnp.zeros((CRS + 1 - INL, 1, NT), jnp.float32)


def conductivity(power):
    return contrast_sq / (contrast_sq + power)


def partial_kernel(axes, vol, narrow1, narrow0, partial, cells_v):
    rank = lax.axis_index(axes[1])
    even = lax.rem(rank, 2) == 0
    col = iota((CRS, NT), 1)
    row = iota((CRS, NT), 0)
    for i in range(INL):
        here = vol[i]
        edge = jnp.where(even, narrow1[i], narrow0[i])
        edge = jnp.where(rank == 0, here[:1], edge)
        lower = jnp.where(row == 0, edge, pltpu.roll(here, 1, 0))
        edge = jnp.where(even, narrow0[i], narrow1[i])
        edge = jnp.where(rank == NARROW - 1, here[CRS - 1 :], edge)
        upper = jnp.where(row == CRS - 1, edge, pltpu.roll(here, CRS - 1, 0))
        power = (0.5 * (upper - lower)) ** 2
        earlier = jnp.where(col == 0, here, pltpu.roll(here, 1, 1))
        later = jnp.where(col == NT - 1, here, pltpu.roll(here, NT - 1, 1))
        power = power + (0.5 * (later - earlier)) ** 2
        if 0 < i < INL - 1:
            power = conductivity(power + (0.5 * (vol[i + 1] - vol[i - 1])) ** 2)
        partial[i] = power
        for t in range(TILES):
            cells_v[pl.ds(i * TILES + t, CRS, stride=ROWS), :] = here[:, lane_tile(t)]


def prepare_kernel(
    axes, vol, partial, cells_v, wide1, wide0, cond, wide_out, narrow_out, cells_c
):
    rank = lax.axis_index(axes[0])
    even = lax.rem(rank, 2) == 0
    for i in range(INL):
        value = partial[i]
        if i == 0:
            up = jnp.where(even, wide1[0], wide0[0])
            up = jnp.where(rank == 0, vol[0], up)
            value = conductivity(value + (0.5 * (vol[1] - up)) ** 2)
        if i == INL - 1:
            down = jnp.where(even, wide0[0], wide1[0])
            down = jnp.where(rank == WIDE - 1, vol[INL - 1], down)
            value = conductivity(value + (0.5 * (down - vol[INL - 2])) ** 2)
        cond[i] = value
        for t in range(TILES):
            where = pl.ds(i * TILES + t, CRS, stride=ROWS)
            cells_c[where, :] = value[:, lane_tile(t)]
    ones = jnp.ones((ROWS, LANES), jnp.float32)
    v = [cells_v[pl.ds(c * ROWS, ROWS), :] for c in range(CRS)]
    k = [cells_c[pl.ds(c * ROWS, ROWS), :] for c in range(CRS)]
    m0, d0, m1, d1, g, _ = condense([ones] * CRS, v, links(k))
    for p, value in enumerate((g, m0, m1, d0, d1, k[0], k[-1])):
        narrow_out[p * ROWS : (p + 1) * ROWS, :] = value
    ones = jnp.ones((GROUP, LANES), jnp.float32)
    for t in range(TILES):
        for u in range(CRS // GROUP):
            at = (slice(u * GROUP, (u + 1) * GROUP), lane_tile(t))
            v = [vol[(i, *at)] for i in range(INL)]
            k = [cond[(i, *at)] for i in range(INL)]
            _, d0, _, d1, _, _ = condense([ones] * INL, v, links(k))
            for p, value in enumerate((*k, d0, d1)):
                start = t * GROUP * 2 * WPORTS + p * 2 + u
                wide_out[pl.ds(start, GROUP, stride=2 * WPORTS), :] = value


def sublane_shift(x, s):
    return pltpu.roll(x, s % GROUP, 0)


def wide_kernel(ports, out):
    part = WIDE // GROUP
    sub = iota((GROUP, LANES), 0)
    zero = jnp.zeros((GROUP, LANES), jnp.float32)
    ones = jnp.ones((GROUP, LANES), jnp.float32)
    for u in range(2):

        def port(p, j):
            return ports[pl.ds(j * 2 * WPORTS + p * 2 + u, GROUP, stride=part * 2 * WPORTS), :]

        last_cond = sublane_shift(port(INL - 1, part - 1), 1)
        mass, rhs, link = [zero], [zero], []
        for j in range(part):
            k = [port(p, j) for p in range(INL)]
            joined = half_weight * (last_cond + k[0])
            if j == 0:
                joined = jnp.where(sub == 0, 0.0, joined)
            m0, _, m1, _, g, _ = condense([ones] * INL, [zero] * INL, links(k))
            link += [joined, g]
            mass += [m0, m1]
            rhs += [port(INL, j), port(INL + 1, j)]
            last_cond = k[-1]
        count = len(mass)
        m0, d0, m1, d1, g, steps = condense(mass, rhs, link)
        last = halving(
            m1 + sublane_shift(m0, -1),
            d1 + sublane_shift(d0, -1),
            g,
            sublane_shift(g, -1),
            sublane_shift,
            GROUP,
        )
        x = expand(sublane_shift(last, 1), last, steps, count)
        for j in range(part):
            for e in range(2):
                out[pl.ds(j * 4 + e * 2 + u, GROUP, stride=part * 4), :] = x[1 + 2 * j + e]


def time_kernel(vol, cond, out, inner, cells_v, cells_c, link_s, tmp):
    ones = jnp.ones((GROUP, LANES), jnp.float32)
    for t in range(TILES):
        for u in range(CRS // GROUP):
            at = (slice(u * GROUP, (u + 1) * GROUP), lane_tile(t))
            v = [vol[(i, *at)] for i in range(INL)]
            k = [cond[(i, *at)] for i in range(INL)]
            near, far = condense([ones] * INL, v, links(k))[-1]
            _, _, _, a1, c1, b1 = near
            _, _, _, a2, c2, b2 = far
            found = (b1 + c1 * b2, a1 + c1 * a2, c1 * c2, b2, a2, c2)
            for p, value in enumerate(found):
                inner[(p, *at)] = value
    lines = INL * CRS
    half = NT // 2
    blocks = half // LANES
    for b in range(blocks):
        for source, cells in ((vol, cells_v), (cond, cells_c)):
            stacked = jnp.concatenate(
                [
                    source[:, :, b * LANES : (b + 1) * LANES].reshape(lines, LANES),
                    source[:, :, half + b * LANES : half + (b + 1) * LANES].reshape(lines, LANES),
                ],
                0,
            )
            cells[b * LANES : (b + 1) * LANES, :] = stacked.T
    lane = iota((GROUP, LANES), 1)
    sub = iota((GROUP, LANES), 0)
    low = lane < lines

    def swap(x):
        return pltpu.roll(x, lines, 1)

    for s in range(half // GROUP):
        here = cells_c[s * GROUP : (s + 1) * GROUP, :]
        if s:
            edge = cells_c[s * GROUP - 1 : s * GROUP, :]
        else:
            edge = swap(cells_c[half - GROUP : half, :])[GROUP - 1 :]
        value = half_weight * (here + jnp.where(sub == 0, edge, pltpu.roll(here, 1, 0)))
        if s == 0:
            value = jnp.where((sub == 0) & low, 0.0, value)
        link_s[s * GROUP : (s + 1) * GROUP, :] = value

    def chain_shift(x, s):
        n = x.shape[0]
        if abs(s) == n:
            return swap(x)
        rolled = pltpu.roll(x, s % n, 0)
        place = iota(x.shape, 0)
        wrapped = place < s if s > 0 else place >= n + s
        return jnp.where(wrapped, swap(rolled), rolled)

    runs = half // GROUP
    zero = jnp.zeros((runs, LANES), jnp.float32)
    ones = jnp.ones((runs, LANES), jnp.float32)
    v = [cells_v[pl.ds(k, runs, stride=GROUP), :] for k in range(GROUP)]
    link = [link_s[pl.ds(k, runs, stride=GROUP), :] for k in range(GROUP)]
    m0, d0, m1, d1, g, steps = condense([zero] + [ones] * GROUP, [zero] + v, link)
    tmp[0] = m1 + chain_shift(m0, -1)
    tmp[1] = d1 + chain_shift(d0, -1)
    tmp[2] = g
    zero = jnp.zeros((GROUP, LANES), jnp.float32)

    def take(p):
        return [tmp[p, pl.ds(k, GROUP, stride=GROUP), :] for k in range(GROUP)]

    m0, d0, m1, d1, g, inner = condense([zero] + take(0), [zero] + take(1), take(2))
    last = halving(
        m1 + chain_shift(m0, -1),
        d1 + chain_shift(d0, -1),
        g,
        chain_shift(g, -1),
        chain_shift,
        2 * GROUP,
    )
    x = expand(chain_shift(last, 1), last, inner, GROUP + 1)
    for k in range(GROUP):
        tmp[0, pl.ds(k, GROUP, stride=GROUP), :] = x[k + 1]
    last = tmp[0]
    x = expand(chain_shift(last, 1), last, steps, GROUP + 1)
    for k in range(GROUP):
        cells_v[pl.ds(k, runs, stride=GROUP), :] = x[k + 1]
    for b in range(blocks):
        turned = cells_v[b * LANES : (b + 1) * LANES, :].T
        for h in range(2):
            out[:, :, h * half + b * LANES : h * half + (b + 1) * LANES] = turned[
                h * lines : (h + 1) * lines
            ].reshape(INL, CRS, LANES)


def ports_of(ref):
    return [ref[p * ROWS : (p + 1) * ROWS, :] for p in range(PORTS)]


def chain_of(ports):
    mass, rhs, link = [], [], []
    for n, (g, m0, m1, d0, d1, _, _) in enumerate(ports):
        mass += [m0, m1]
        rhs += [d0, d1]
        link.append(g)
        if n < len(ports) - 1:
            link.append(half_weight * (ports[n][6] + ports[n + 1][5]))
    return mass, rhs, link


def in_order(mine, theirs, first):
    return [
        [jnp.where(first, a, b) for a, b in zip(mine, theirs)],
        [jnp.where(first, b, a) for a, b in zip(mine, theirs)],
    ]


def places(axes):
    rank = lax.axis_index(axes[1])
    return lax.rem(rank, 2) == 0, lax.rem(rank, RUN) < 2, rank < RUN


def join_kernel(axes, own, beside, joined):
    pair = in_order(ports_of(own), ports_of(beside), places(axes)[0])
    m0, d0, m1, d1, g, _ = condense(*chain_of(pair))
    for p, value in enumerate((g, m0, m1, d0, d1, pair[0][5], pair[1][6])):
        joined[p * ROWS : (p + 1) * ROWS, :] = value


def facing(run, low):
    m0, d0, m1, d1, g, steps = condense(*chain_of(run))
    here_m, here_d = jnp.where(low, m1, m0), jnp.where(low, d1, d0)
    away_m, away_d = jnp.where(low, m0, m1), jnp.where(low, d0, d1)
    inverse = 1.0 / (g + away_m)
    slope, base = g * inverse, away_d * inverse
    edge = (here_m + slope * away_m, here_d + slope * away_d, jnp.where(low, run[-1][6], run[0][5]))
    return (slope, base, steps), edge


def edge_kernel(axes, joined, across, out):
    _, second, low = places(axes)
    _, edge = facing(in_order(ports_of(joined), ports_of(across), second), low)
    for p, value in enumerate(edge):
        out[p * ROWS : (p + 1) * ROWS, :] = value


def half_of(x, first):
    return jnp.where(first, x[0], x[2]), jnp.where(first, x[1], x[3])


def cross_kernel(
    axes, own, beside, joined, across, other, cells_v, cells_c, timed, out, cells_x
):
    first, second, low = places(axes)
    run = in_order(ports_of(joined), ports_of(across), second)
    (slope, base, steps), (m0, d0, c0) = facing(run, low)
    m1, d1, c1 = [other[p * ROWS : (p + 1) * ROWS, :] for p in range(3)]
    link = half_weight * (c0 + c1)
    here = (d0 * (m1 + link) + link * d1) / (m0 * m1 + link * (m0 + m1))
    away = base + slope * here
    x = expand(jnp.where(low, away, here), jnp.where(low, here, away), steps, 4)
    steps = condense(*chain_of(in_order(ports_of(own), ports_of(beside), first)))[-1]
    x = expand(*half_of(x, second), steps, 4)
    v = [cells_v[pl.ds(c * ROWS, ROWS), :] for c in range(CRS)]
    k = [cells_c[pl.ds(c * ROWS, ROWS), :] for c in range(CRS)]
    ones = jnp.ones((ROWS, LANES), jnp.float32)
    steps = condense([ones] * CRS, v, links(k))[-1]
    x = expand(*half_of(x, first), steps, CRS)
    for c in range(CRS):
        cells_x[c * ROWS : (c + 1) * ROWS, :] = x[c]
    for i in range(INL):
        for t in range(TILES):
            out[i, :, lane_tile(t)] = (
                timed[i, :, lane_tile(t)] + cells_x[pl.ds(i * TILES + t, CRS, stride=ROWS), :]
            )


def finish_kernel(inner, ends, others, out):
    for t in range(TILES):
        for u in range(CRS // GROUP):
            at = (slice(u * GROUP, (u + 1) * GROUP), lane_tile(t))
            first = ends[pl.ds(t * GROUP * 4 + u, GROUP, stride=4), :]
            last = ends[pl.ds(t * GROUP * 4 + 2 + u, GROUP, stride=4), :]
            base, to_first, to_last, base2, to_first2, to_last2 = [
                inner[(p, *at)] for p in range(6)
            ]
            second = base + to_first * first + to_last * last
            third = base2 + to_first2 * first + to_last2 * last
            for i, x in enumerate((first, second, third, last)):
                out[(i, *at)] = (x + others[(i, *at)]) * (1.0 / 3.0)


def f32(*shape):
    return jax.ShapeDtypeStruct(shape, jnp.float32)


def call(kernel, out, *args, scratch=()):
    return pl.pallas_call(
        kernel,
        out_shape=out,
        scratch_shapes=[pltpu.VMEM(s, jnp.float32) for s in scratch],
        compiler_params=pltpu.CompilerParams(vmem_limit_bytes=16 * 2**20),
    )(*args)


def per_device(axes, volume):
    wide_axes, narrow_axes = axes

    def exchanged(layer, axis, count, start):
        pairs = [(i, i + 1) for i in range(start, count - 1, 2)]
        return lax.ppermute(layer, axis, pairs + [(j, i) for i, j in pairs])

    inline_face, longer = f32(1, CRS, NT), f32(CRS + 1, 1, NT)
    narrow1, wide1, narrow0, wide0 = call(
        lambda *refs: faces_kernel(axes, *refs),
        (longer, inline_face, longer, inline_face),
        volume,
    )
    narrow1 = exchanged(narrow1, narrow_axes, NARROW, 1)
    wide1 = exchanged(wide1, wide_axes, WIDE, 1)
    narrow0 = exchanged(narrow0, narrow_axes, NARROW, 0)
    wide0 = exchanged(wide0, wide_axes, WIDE, 0)
    cells = CRS * ROWS
    partial, cells_v = call(
        lambda *refs: partial_kernel(axes, *refs),
        (f32(INL, CRS, NT), f32(cells, LANES)),
        volume,
        narrow1,
        narrow0,
    )
    cond, wide_ports, narrow_ports, cells_c = call(
        lambda *refs: prepare_kernel(axes, *refs),
        (
            f32(INL, CRS, NT),
            f32(WIDE * WPORTS * 2, LANES),
            f32(PORTS * ROWS, LANES),
            f32(cells, LANES),
        ),
        volume,
        partial,
        cells_v,
        wide1,
        wide0,
    )
    lines = lax.all_to_all(
        wide_ports.reshape(WIDE, WPORTS, 2, LANES), wide_axes, split_axis=0, concat_axis=0, tiled=True
    )

    def swapped(x, step):
        return lax.ppermute(x, narrow_axes, [(n, n ^ step) for n in range(NARROW)])

    beside = swapped(narrow_ports, 1)
    joined = call(
        lambda *refs: join_kernel(axes, *refs), f32(PORTS * ROWS, LANES), narrow_ports, beside
    )
    across = swapped(joined, 3)
    edge = call(lambda *refs: edge_kernel(axes, *refs), f32(3 * ROWS, LANES), joined, across)
    other = swapped(edge, RUN)
    timed, inner = call(
        time_kernel,
        (f32(INL, CRS, NT), f32(6, CRS, NT)),
        volume,
        cond,
        scratch=(
            (NT // 2, LANES),
            (NT // 2, LANES),
            (NT // 2, LANES),
            (3, NT // 2 // GROUP, LANES),
        ),
    )
    lines, edge, timed = lax.optimization_barrier((lines, edge, timed))
    solved = call(
        wide_kernel, f32(WIDE * 4, LANES), lines.reshape(WIDE * WPORTS * 2, LANES)
    )
    ends = lax.all_to_all(
        solved.reshape(WIDE, 2, 2, LANES), wide_axes, split_axis=0, concat_axis=0, tiled=True
    )
    others = call(
        lambda *refs: cross_kernel(axes, *refs),
        f32(INL, CRS, NT),
        narrow_ports,
        beside,
        joined,
        across,
        other,
        cells_v,
        cells_c,
        timed,
        scratch=((cells, LANES),),
    )
    return call(
        finish_kernel, f32(INL, CRS, NT), inner, ends.reshape(WIDE * 4, LANES), others
    )


def solution(mesh):
    axes = ("wide", "narrow")
    return jax.shard_map(
        lambda volume: per_device(axes, volume),
        mesh=mesh,
        in_specs=(P("wide", "narrow", None),),
        out_specs=P("wide", "narrow", None),
        check_vma=False,
    )
```
